512 devices in a mesh: dp: 64 (over x, z_hi, y, core), fsdp: 8 (over z_lo).
Axes of the slice: x: 4, y: 4, z: 16 (z_hi: 2, z_lo: 8; z = z_hi * 8 + z_lo), core: 2. Of those that a mesh axis runs over, the one named last changes fastest.
Arguments:
- inputs: bfloat16 [49152, 8192], P('dp', 'fsdp'), may hold values from -6 to 6
- grad_out: bfloat16 [49152, 14336], P('dp', 'fsdp'), may hold values from -0.078125 to 0.078125
- projector: bfloat16 [8192, 256], P('fsdp', 'dp'), may hold values from -0.0625 to 0.0625
- moment: float32 [14336, 256], P(('fsdp', 'dp')), may hold values from -3 to 3
- second: float32 [14336, 256], P(('fsdp', 'dp')), may hold values from 0.05 to 2
Outputs:
- update: bfloat16 [8, 1792, 8192], P(None, 'dp', 'fsdp')
- moment_new: float32 [14336, 256], P(('fsdp', 'dp'))
- second_new: float32 [14336, 256], P(('fsdp', 'dp'))
The draws below stay inside these ranges and needn't reach their ends.
All inputs are finite; a program needn't handle non-finite values.
Results may differ from the reference program's by a relative error of at most 0.005.
Values may be sent and summed in bfloat16 or wider, within the bound.
A program may use at most 64 MiB of HBM per device.

```python
import math
import jax
import jax.numpy as jnp
from jax import lax

D = 8192
FW = 14336
R = 256
STEP = 10
TOKENS = 49152
FB = 1792
N_FSDP = 8


def strengthened(drawn, key, source, target, shards_of, factor):
    def block_of(position):
        return (jnp.arange(drawn.shape[position]) // (drawn.shape[position] // shards_of)).reshape((-1,) + (1,) * (drawn.ndim - 1 - position))

    one_side = jax.random.permutation(key, shards_of)[block_of(target)]
    far = (block_of(target) + shards_of // 2) % shards_of
    return jnp.where((block_of(source) == one_side) | (block_of(source) == far), factor * drawn, drawn)


def level_of(rng, shape, split, smallest, largest):
    def one(axis_at, parts):
        heights = jax.random.uniform(jax.random.fold_in(jax.random.fold_in(rng, 6), axis_at), (parts,), jnp.float32, smallest / len(split), largest / len(split))
        return jnp.repeat(jnp.exp(heights), shape[axis_at] // parts).reshape((-1,) + (1,) * (len(shape) - axis_at - 1))

    gain = one(*split[0])
    for cut in split[1:]:
        gain = gain * one(*cut)
    return gain


def gaussian(stream_key, extent, deviation, reach, cuts=(), kind=jnp.bfloat16):
    drawn = jax.random.normal(stream_key, extent, jnp.float32) * deviation
    if len(cuts) > 0:
        drawn = level_of(stream_key, extent, cuts, -0.22, 0.18) * drawn
    return jnp.clip(drawn, min=-reach, max=reach).astype(kind)


def bell_draw_with(stream_key, extent, spread, limit, pieces, heavy, dtype=jnp.bfloat16):
    entries = spread * jax.random.normal(stream_key, extent, jnp.float32)
    if pieces:
        entries = entries * level_of(stream_key, extent, pieces, -0.22, 0.18)
    return jnp.clip(strengthened(entries, jax.random.fold_in(stream_key, 3), *heavy), -limit, limit).astype(dtype)


def setup_inputs(seed: int = 0) -> dict:
    key_of = jax.random.split(jax.random.key(seed), 6)
    return {
        "inputs": gaussian(key_of[0], (TOKENS, D), 1.0, 6.0, ((0, 64), (1, 8))),
        "grad_out": bell_draw_with(key_of[1], (TOKENS, FW), (TOKENS ** -0.5), 0.078125, ((0, 64), (1, 8)), (0, 1, 64, 4.0)),
        "projector": gaussian(key_of[2], (D, R), D ** -0.5, 0.0625, ((0, 8), (1, 64))),
        "moment": gaussian(key_of[3], (FW, R), 0.5, 3.0, ((0, 512),), jnp.float32),
        "second": jnp.clip(jnp.exp(math.log(2.0) - 3.6888794 * jax.random.uniform(key_of[4], (FW, R), jnp.float32) ** level_of(key_of[4], (FW, R), ((0, 512),), -0.2, 0.2)), 0.05, 2.0),
    }


BETA_FIRST = 0.9
BETA_SECOND = 0.999
EPSILON = 1e-08

def adam_direction(grad_sub, moment, second):
    moment_new = BETA_FIRST * moment + (1.0 - BETA_FIRST) * grad_sub
    second_new = BETA_SECOND * second + (1.0 - BETA_SECOND) * grad_sub * grad_sub
    first_hat = moment_new / (1.0 - BETA_FIRST ** STEP)
    second_hat = second_new / (1.0 - BETA_SECOND ** STEP)
    direction = (first_hat / (jnp.sqrt(second_hat) + EPSILON)).astype(jnp.bfloat16)
    return (moment_new, second_new, direction)

def reference(inputs, grad_out, projector, moment, second):
    projected = jnp.dot(inputs, projector, preferred_element_type=jnp.float32).astype(jnp.bfloat16)
    grad_sub = lax.dot_general(grad_out, projected, (((0,), (0,)), ((), ())), preferred_element_type=jnp.float32)
    moment_new, second_new, direction = adam_direction(grad_sub, moment, second)
    decoded = lax.dot_general(direction, projector, (((1,), (1,)), ((), ())), preferred_element_type=jnp.float32)
    update = decoded.astype(jnp.bfloat16).reshape(N_FSDP, FB, D)
    return (update, moment_new, second_new)
```

```python
import functools

import jax
import jax.numpy as jnp
from jax import lax
from jax.experimental import pallas as pl
from jax.experimental.pallas import tpu as pltpu
from jax.sharding import PartitionSpec as P

MESH = pl.DeviceIdType.MESH
F32 = jnp.float32
BF16 = jnp.bfloat16

STEP = 10
BETA_FIRST = 0.9
BETA_SECOND = 0.999
EPSILON = 1e-08

TOKENS = 768
FEATURES = 1024
UNITS = 1792
RANK = 256
OWNED = 28
PAD = 32
LINE = 8
PIECE = 48
PIECES = TOKENS // PIECE
SKEW = 6


def adam_direction(grad_sub, moment, second):
    moment_new = BETA_FIRST * moment + (1.0 - BETA_FIRST) * grad_sub
    second_new = BETA_SECOND * second + (1.0 - BETA_SECOND) * grad_sub * grad_sub
    first_hat = moment_new / (1.0 - BETA_FIRST**STEP)
    second_hat = second_new / (1.0 - BETA_SECOND**STEP)
    direction = first_hat / (jnp.sqrt(second_hat) + EPSILON)
    return (moment_new, second_new, direction)


def to_natural(v):
    return jnp.concatenate([v[:, zh * 128 + x * 32 : zh * 128 + x * 32 + 32] for x in range(4) for zh in range(2)], axis=1)


def to_halves(v):
    return jnp.concatenate([v[:, x * 64 + zh * 32 : x * 64 + zh * 32 + 32] for zh in range(2) for x in range(4)], axis=1)


def kernel(
    blk, x_hbm, go_hbm, mom, sec,
    upd, mnew, snew,
    x_v, go_v, got, raw, basis, own, pre, suf, out_r, out_l, proj, btf, btb, cbuf, s1, rb, zsend, zrecv, dirs,
    load_sem, z_send, z_recv, g_send, g_recv, c_send, c_recv, r_send, r_recv, l_send, l_recv, b_send, b_recv, d_send, d_recv,
):
    d = lax.axis_index("dp")
    f = lax.axis_index("fsdp")
    core = lax.rem(d, 2)
    y = lax.rem(d // 2, 4)
    zh = lax.rem(d // 8, 2)
    xx = d // 16
    pos = xx * 4 + y
    other_core = (d + 1 - 2 * core, f)
    other_zh = (d + 8 - 16 * zh, f)

    def at_pos(q):
        return (((q // 4) * 2 + zh) * 8 + lax.rem(q, 4) * 2 + core, f)

    load_x = pltpu.make_async_copy(x_hbm, x_v, load_sem.at[0])
    load_go = pltpu.make_async_copy(go_hbm, go_v, load_sem.at[1])
    load_x.start()
    load_go.start()

    barrier = pltpu.get_barrier_semaphore()
    pl.semaphore_signal(barrier, inc=1, device_id=other_zh, device_id_type=MESH)
    pl.semaphore_signal(barrier, inc=1, device_id=other_core, device_id_type=MESH)

    def greet(i, _):
        pl.semaphore_signal(barrier, inc=1, device_id=at_pos(lax.rem(pos + i, 16)), device_id_type=MESH)
        return 0

    lax.fori_loop(1, 16, greet, 0)

    def greet_line(i, _):
        pl.semaphore_signal(barrier, inc=1, device_id=(d, lax.rem(f + i, LINE)), device_id_type=MESH)
        return 0

    lax.fori_loop(1, LINE, greet_line, 0)
    raw[zh, core, pos] = blk[...]
    pl.semaphore_wait(barrier, 24)

    def send_block(which, i):
        q = lax.rem(pos + i, 16)
        return pltpu.make_async_remote_copy(
            raw.at[which, core, pos], raw.at[which, core, pos], g_send.at[which, i], g_recv.at[which, pos],
            device_id=at_pos(q), device_id_type=MESH)

    def wait_block(which, i):
        q = lax.rem(pos + 16 - i, 16)
        pltpu.make_async_remote_copy(
            raw.at[which, core, q], raw.at[which, core, q], g_send.at[which, i], g_recv.at[which, q],
            device_id=at_pos(q), device_id_type=MESH).wait_recv()

    def each_peer(action):
        def body(i, _):
            action(i)
            return 0
        lax.fori_loop(1, 16, body, 0)

    swap_zh = pltpu.make_async_remote_copy(
        raw.at[zh, core, pos], raw.at[zh, core, pos], z_send.at[0], z_recv.at[0], device_id=other_zh, device_id_type=MESH)
    swap_zh.start()
    each_peer(lambda i: send_block(zh, i).start())

    def swap_core(which):
        return pltpu.make_async_remote_copy(
            raw.at[which, core], raw.at[which, core], c_send.at[which], c_recv.at[which],
            device_id=other_core, device_id_type=MESH)

    load_go.wait()

    def turn(i, _):
        cols = pl.ds(pl.multiple_of(i * 128, 128), 128)
        got[cols, :] = go_v[:, cols].T
        return 0

    lax.fori_loop(0, UNITS // 128, turn, 0)

    each_peer(lambda i: wait_block(zh, i))
    swap_core(zh).start()
    swap_zh.wait_recv()
    each_peer(lambda i: send_block(1 - zh, i).start())

    row = lax.broadcasted_iota(jnp.int32, (256, 256), 0)
    col = lax.broadcasted_iota(jnp.int32, (256, 256), 1)
    source = ((row // 4) % 2) * 128 + ((row // 8) % 4) * 32 + (row // 32) * 4 + row % 4
    perm = jnp.where(col == source, 1.0, 0.0).astype(BF16)

    def unfold(which):
        for x in range(4):
            blocks = jnp.concatenate(
                [raw[which, 0, 4 * x : 4 * x + 4].reshape(128, 128), raw[which, 1, 4 * x : 4 * x + 4].reshape(128, 128)], axis=0)
            placed = jnp.dot(perm, blocks, preferred_element_type=F32).astype(BF16)
            for b in range(8):
                basis[which, 32 * x : 32 * x + 32, 128 * b : 128 * b + 128] = placed[32 * b : 32 * b + 32]

    def project(which):
        half = pl.ds(pl.multiple_of(which * 128, 128), 128)
        own[:, half] = lax.dot_general(
            x_v[...], basis[which], (((1,), (1,)), ((), ())), preferred_element_type=F32)

    load_x.wait()
    swap_core(zh).wait()
    unfold(zh)
    project(zh)
    each_peer(lambda i: wait_block(1 - zh, i))
    swap_core(1 - zh).start()
    swap_core(1 - zh).wait()
    unfold(1 - zh)
    project(1 - zh)
    swap_zh.wait_send()
    each_peer(lambda i: send_block(zh, i).wait_send())
    each_peer(lambda i: send_block(1 - zh, i).wait_send())

    @pl.when(f == 0)
    def _():
        pre[...] = jnp.zeros_like(pre)

    @pl.when(f == LINE - 1)
    def _():
        suf[...] = jnp.zeros_like(suf)

    def right(p):
        rows = pl.ds(pl.multiple_of(p * PIECE, PIECE), PIECE)
        return pltpu.make_async_remote_copy(
            out_r.at[rows], pre.at[rows], r_send.at[p], r_recv.at[p],
            device_id=(d, lax.rem(f + 1, LINE)), device_id_type=MESH)

    def left(p):
        rows = pl.ds(pl.multiple_of(p * PIECE, PIECE), PIECE)
        return pltpu.make_async_remote_copy(
            out_l.at[rows], suf.at[rows], l_send.at[p], l_recv.at[p],
            device_id=(d, lax.rem(f + LINE - 1, LINE)), device_id_type=MESH)

    def step(t, _):
        p = t - f * SKEW

        @pl.when((p >= 0) & (p < PIECES))
        def _():
            @pl.when(f > 0)
            def _():
                right(p).wait_recv()

            @pl.when(f < LINE - 1)
            def _():
                rows = pl.ds(pl.multiple_of(p * PIECE, PIECE), PIECE)
                out_r[rows] = (own[rows] + pre[rows].astype(F32)).astype(BF16)
                right(p).start()

        q = t - (LINE - 1 - f) * SKEW

        @pl.when((q >= 0) & (q < PIECES))
        def _():
            @pl.when(f < LINE - 1)
            def _():
                left(q).wait_recv()

            @pl.when(f > 0)
            def _():
                rows = pl.ds(pl.multiple_of(q * PIECE, PIECE), PIECE)
                out_l[rows] = (own[rows] + suf[rows].astype(F32)).astype(BF16)
                left(q).start()

        return 0

    lax.fori_loop(0, PIECES + (LINE - 1) * SKEW, step, 0)

    proj[...] = (own[...] + (pre[...].astype(F32) + suf[...].astype(F32))).astype(BF16)

    btf[UNITS:, :] = jnp.zeros((8, RANK), F32)

    def terms(i, _):
        rows = pl.ds(pl.multiple_of(i * 448, 448), 448)
        btf[rows, :] = jnp.dot(got[rows, :], proj[...], preferred_element_type=F32)
        return 0

    lax.fori_loop(0, UNITS // 448, terms, 0)

    def place(i, _):
        two = btf[pl.ds(pl.multiple_of(i * 56, 8), 64), :]
        j = ((i // 8) * 4 + lax.rem(i, 4)) * 2 + lax.rem(i // 4, 2)
        btb[0, j] = two[:PAD].astype(BF16)
        btb[1, j] = pltpu.roll(two, 64 - OWNED, 0)[:PAD].astype(BF16)
        return 0

    lax.fori_loop(0, 32, place, 0)

    swap_terms = pltpu.make_async_remote_copy(
        btb.at[1 - core], cbuf, c_send.at[2], c_recv.at[2], device_id=other_core, device_id_type=MESH)
    swap_terms.start()
    swap_terms.wait()

    def add_cores(i, _):
        s1[i] = (btb[core, i].astype(F32) + cbuf[i].astype(F32)).astype(BF16)
        return 0

    lax.fori_loop(0, 32, add_cores, 0)

    def send_terms(i):
        q = lax.rem(pos + i, 16)
        return pltpu.make_async_remote_copy(
            s1.at[pl.ds(q * 2, 2)], rb.at[pos], b_send.at[i], b_recv.at[pos], device_id=at_pos(q), device_id_type=MESH)

    each_peer(lambda i: send_terms(i).start())

    def add_terms(i, acc):
        q = lax.rem(pos + 16 - i, 16)
        pltpu.make_async_remote_copy(
            s1.at[pl.ds(q * 2, 2)], rb.at[q], b_send.at[i], b_recv.at[q],
            device_id=at_pos(q), device_id_type=MESH).wait_recv()
        return (acc[0] + rb[q, zh].astype(F32), acc[1] + rb[q, 1 - zh].astype(F32))

    mine, theirs = lax.fori_loop(
        1, 16, add_terms, (s1[2 * pos + zh].astype(F32), s1[2 * pos + 1 - zh].astype(F32)))
    zsend[...] = theirs.astype(BF16)
    swap_sum = pltpu.make_async_remote_copy(
        zsend, zrecv, z_send.at[1], z_recv.at[1], device_id=other_zh, device_id_type=MESH)
    swap_sum.start()
    swap_sum.wait()
    grad_sub = to_natural(mine + zrecv[...].astype(F32))

    moment_new, second_new, direction = adam_direction(grad_sub, mom[...], sec[...])
    mnew[...] = moment_new[:OWNED]
    snew[...] = second_new[:OWNED]
    dirs[f] = to_halves(direction).astype(BF16)

    def send_dir(i):
        return pltpu.make_async_remote_copy(
            dirs.at[f], dirs.at[f], d_send.at[i], d_recv.at[f],
            device_id=(d, lax.rem(f + i, LINE)), device_id_type=MESH)

    def each_line(action):
        def body(i, _):
            action(i)
            return 0
        lax.fori_loop(1, LINE, body, 0)

    each_line(lambda i: send_dir(i).start())

    def wait_dir(i):
        q = lax.rem(f + LINE - i, LINE)
        pltpu.make_async_remote_copy(
            dirs.at[q], dirs.at[q], d_send.at[i], d_recv.at[q], device_id=(d, q), device_id_type=MESH).wait_recv()

    each_line(wait_dir)
    both = basis[...].reshape(RANK, FEATURES)
    upd[...] = jnp.dot(
        dirs[...].reshape(LINE * PAD, RANK), both, preferred_element_type=F32).astype(BF16)

    each_peer(lambda i: send_terms(i).wait_send())
    each_line(lambda i: send_dir(i).wait_send())

    def sent(p, _):
        @pl.when(f < LINE - 1)
        def _():
            right(p).wait_send()

        @pl.when(f > 0)
        def _():
            left(p).wait_send()

        return 0

    lax.fori_loop(0, PIECES, sent, 0)


def local(inputs, grad_out, projector, moment, second):
    blk = projector.T.reshape(4, 8, 128).transpose(1, 0, 2).reshape(32, 128)
    grow = ((0, PAD - OWNED), (0, 0))
    vmem = pl.BlockSpec(memory_space=pltpu.VMEM)
    anywhere = pl.BlockSpec(memory_space=pl.ANY)
    dma = pltpu.SemaphoreType.DMA
    update, moment_new, second_new = pl.pallas_call(
        kernel,
        out_shape=(
            jax.ShapeDtypeStruct((LINE * PAD, FEATURES), BF16),
            jax.ShapeDtypeStruct((OWNED, RANK), F32),
            jax.ShapeDtypeStruct((OWNED, RANK), F32),
        ),
        in_specs=[vmem, anywhere, anywhere, vmem, vmem],
        out_specs=(vmem, vmem, vmem),
        scratch_shapes=[
            pltpu.VMEM((TOKENS, FEATURES), BF16),
            pltpu.VMEM((TOKENS, UNITS), BF16),
            pltpu.VMEM((UNITS, TOKENS), BF16),
            pltpu.VMEM((2, 2, 16, 32, 128), BF16),
            pltpu.VMEM((2, 128, FEATURES), BF16),
            pltpu.VMEM((TOKENS, RANK), F32),
            pltpu.VMEM((TOKENS, RANK), BF16),
            pltpu.VMEM((TOKENS, RANK), BF16),
            pltpu.VMEM((TOKENS, RANK), BF16),
            pltpu.VMEM((TOKENS, RANK), BF16),
            pltpu.VMEM((TOKENS, RANK), BF16),
            pltpu.VMEM((UNITS + 8, RANK), F32),
            pltpu.VMEM((2, 32, PAD, RANK), BF16),
            pltpu.VMEM((32, PAD, RANK), BF16),
            pltpu.VMEM((32, PAD, RANK), BF16),
            pltpu.VMEM((16, 2, PAD, RANK), BF16),
            pltpu.VMEM((PAD, RANK), BF16),
            pltpu.VMEM((PAD, RANK), BF16),
            pltpu.VMEM((LINE, PAD, RANK), BF16),
            dma((2,)),
            dma((2,)), dma((2,)),
            dma((2, 16)), dma((2, 16)),
            dma((3,)), dma((3,)),
            dma((PIECES,)), dma((PIECES,)), dma((PIECES,)), dma((PIECES,)),
            dma((16,)), dma((16,)),
            dma((LINE,)), dma((LINE,)),
        ],
        compiler_params=pltpu.CompilerParams(
            collective_id=0, has_side_effects=True, vmem_limit_bytes=48 * 1024 * 1024),
    )(blk, inputs, grad_out, jnp.pad(moment, grow), jnp.pad(second, grow, constant_values=1.0))
    return (update.reshape(LINE, PAD, FEATURES)[:, :OWNED], moment_new, second_new)


def solution(mesh):
    return jax.shard_map(
        local,
        mesh=mesh,
        in_specs=(
            P("dp", "fsdp"),
            P("dp", "fsdp"),
            P("fsdp", "dp"),
            P(("fsdp", "dp"), None),
            P(("fsdp", "dp"), None),
        ),
        out_specs=(P(None, "dp", "fsdp"), P(("fsdp", "dp"), None), P(("fsdp", "dp"), None)),
        check_vma=False,
    )
```

```python
import functools

import jax
import jax.numpy as jnp
from jax import lax
from jax.experimental import pallas as pl
from jax.experimental.pallas import tpu as pltpu
from jax.sharding import PartitionSpec as P

MESH = pl.DeviceIdType.MESH
F32 = jnp.float32
BF16 = jnp.bfloat16

STEP = 10
BETA_FIRST = 0.9
BETA_SECOND = 0.999
EPSILON = 1e-08

TOKENS = 768
FEATURES = 1024
UNITS = 1792
RANK = 256
OWNED = 28
PAD = 32
LINE = 8
PIECE = 48
PIECES = TOKENS // PIECE
SKEW = 6


def adam_direction(grad_sub, moment, second):
    moment_new = BETA_FIRST * moment + (1.0 - BETA_FIRST) * grad_sub
    second_new = BETA_SECOND * second + (1.0 - BETA_SECOND) * grad_sub * grad_sub
    first_hat = moment_new / (1.0 - BETA_FIRST**STEP)
    second_hat = second_new / (1.0 - BETA_SECOND**STEP)
    direction = first_hat / (jnp.sqrt(second_hat) + EPSILON)
    return (moment_new, second_new, direction)


def to_natural(v):
    return jnp.concatenate([v[:, zh * 128 + x * 32 : zh * 128 + x * 32 + 32] for x in range(4) for zh in range(2)], axis=1)


def to_halves(v):
    return jnp.concatenate([v[:, x * 64 + zh * 32 : x * 64 + zh * 32 + 32] for zh in range(2) for x in range(4)], axis=1)


def kernel(
    blk, x_hbm, go_hbm, mom_hbm, sec_hbm,
    upd, mnew, snew,
    x_v, go_v, mom, sec, got, raw, basis, own, pre, suf, out_r, out_l, proj, btf, btb, cbuf, s1, rb, zsend, zrecv, direct, dirs,
    load_sem, z_send, z_recv, g_send, g_recv, c_send, c_recv, r_send, r_recv, l_send, l_recv, b_send, b_recv, d_send, d_recv, t_send, t_recv,
):
    d = lax.axis_index("dp")
    f = lax.axis_index("fsdp")
    core = lax.rem(d, 2)
    y = lax.rem(d // 2, 4)
    zh = lax.rem(d // 8, 2)
    xx = d // 16
    pos = xx * 4 + y
    other_core = (d + 1 - 2 * core, f)
    other_zh = (d + 8 - 16 * zh, f)

    def at_pos(q):
        return (((q // 4) * 2 + zh) * 8 + lax.rem(q, 4) * 2 + core, f)

    load_x = pltpu.make_async_copy(x_hbm, x_v, load_sem.at[0])
    load_go = pltpu.make_async_copy(go_hbm, go_v, load_sem.at[1])
    load_mom = pltpu.make_async_copy(mom_hbm, mom, load_sem.at[2])
    load_sec = pltpu.make_async_copy(sec_hbm, sec, load_sem.at[3])
    load_go.start()
    load_x.start()
    load_mom.start()
    load_sec.start()

    barrier = pltpu.get_barrier_semaphore()
    pl.semaphore_signal(barrier, inc=1, device_id=other_zh, device_id_type=MESH)
    pl.semaphore_signal(barrier, inc=1, device_id=other_core, device_id_type=MESH)

    def greet(i, _):
        pl.semaphore_signal(barrier, inc=1, device_id=at_pos(lax.rem(pos + i, 16)), device_id_type=MESH)
        return 0

    lax.fori_loop(1, 16, greet, 0)

    def greet_line(i, _):
        pl.semaphore_signal(barrier, inc=1, device_id=(d, lax.rem(f + i, LINE)), device_id_type=MESH)
        return 0

    lax.fori_loop(1, LINE, greet_line, 0)
    raw[zh, core, pos] = blk[...]
    load_go.wait()

    def turn(i, _):
        cols = pl.ds(pl.multiple_of(i * 128, 128), 128)
        got[cols, :] = go_v[:, cols].T
        return 0

    lax.fori_loop(0, UNITS // 128, turn, 0)

    load_x.wait()
    load_mom.wait()
    load_sec.wait()
    pl.semaphore_wait(barrier, 24)

    def send_block(which, i):
        q = lax.rem(pos + i, 16)
        return pltpu.make_async_remote_copy(
            raw.at[which, core, pos], raw.at[which, core, pos], g_send.at[which, i], g_recv.at[which, pos],
            device_id=at_pos(q), device_id_type=MESH)

    def wait_block(which, i):
        q = lax.rem(pos + 16 - i, 16)
        pltpu.make_async_remote_copy(
            raw.at[which, core, q], raw.at[which, core, q], g_send.at[which, i], g_recv.at[which, q],
            device_id=at_pos(q), device_id_type=MESH).wait_recv()

    def each_peer(action):
        def body(i, _):
            action(i)
            return 0
        lax.fori_loop(1, 16, body, 0)

    swap_zh = pltpu.make_async_remote_copy(
        raw.at[zh, core, pos], raw.at[zh, core, pos], z_send.at[0], z_recv.at[0], device_id=other_zh, device_id_type=MESH)
    swap_zh.start()
    each_peer(lambda i: send_block(zh, i).start())

    def swap_core(which):
        return pltpu.make_async_remote_copy(
            raw.at[which, core], raw.at[which, core], c_send.at[which], c_recv.at[which],
            device_id=other_core, device_id_type=MESH)

    each_peer(lambda i: wait_block(zh, i))
    swap_core(zh).start()
    swap_zh.wait_recv()
    each_peer(lambda i: send_block(1 - zh, i).start())

    row = lax.broadcasted_iota(jnp.int32, (256, 256), 0)
    col = lax.broadcasted_iota(jnp.int32, (256, 256), 1)
    source = ((row // 4) % 2) * 128 + ((row // 8) % 4) * 32 + (row // 32) * 4 + row % 4
    perm = jnp.where(col == source, 1.0, 0.0).astype(BF16)

    def unfold(which):
        for x in range(4):
            blocks = jnp.concatenate(
                [raw[which, 0, 4 * x : 4 * x + 4].reshape(128, 128), raw[which, 1, 4 * x : 4 * x + 4].reshape(128, 128)], axis=0)
            placed = jnp.dot(perm, blocks, preferred_element_type=F32).astype(BF16)
            for b in range(8):
                basis[which, 32 * x : 32 * x + 32, 128 * b : 128 * b + 128] = placed[32 * b : 32 * b + 32]

    def project(which):
        half = pl.ds(pl.multiple_of(which * 128, 128), 128)
        own[:, half] = lax.dot_general(
            x_v[...], basis[which], (((1,), (1,)), ((), ())), preferred_element_type=F32)

    swap_core(zh).wait()
    unfold(zh)
    project(zh)
    each_peer(lambda i: wait_block(1 - zh, i))
    swap_core(1 - zh).start()
    swap_core(1 - zh).wait()
    unfold(1 - zh)
    project(1 - zh)
    swap_zh.wait_send()
    each_peer(lambda i: send_block(zh, i).wait_send())
    each_peer(lambda i: send_block(1 - zh, i).wait_send())

    @pl.when(f == 0)
    def _():
        pre[...] = jnp.zeros_like(pre)

    @pl.when(f == LINE - 1)
    def _():
        suf[...] = jnp.zeros_like(suf)

    def right(p):
        rows = pl.ds(pl.multiple_of(p * PIECE, PIECE), PIECE)
        return pltpu.make_async_remote_copy(
            out_r.at[rows], pre.at[rows], r_send.at[p], r_recv.at[p],
            device_id=(d, lax.rem(f + 1, LINE)), device_id_type=MESH)

    def left(p):
        rows = pl.ds(pl.multiple_of(p * PIECE, PIECE), PIECE)
        return pltpu.make_async_remote_copy(
            out_l.at[rows], suf.at[rows], l_send.at[p], l_recv.at[p],
            device_id=(d, lax.rem(f + LINE - 1, LINE)), device_id_type=MESH)

    def step(t, _):
        p = t - f * SKEW

        @pl.when((p >= 0) & (p < PIECES))
        def _():
            @pl.when(f > 0)
            def _():
                right(p).wait_recv()

            @pl.when(f < LINE - 1)
            def _():
                rows = pl.ds(pl.multiple_of(p * PIECE, PIECE), PIECE)
                out_r[rows] = (own[rows] + pre[rows].astype(F32)).astype(BF16)
                right(p).start()

        q = t - (LINE - 1 - f) * SKEW

        @pl.when((q >= 0) & (q < PIECES))
        def _():
            @pl.when(f < LINE - 1)
            def _():
                left(q).wait_recv()

            @pl.when(f > 0)
            def _():
                rows = pl.ds(pl.multiple_of(q * PIECE, PIECE), PIECE)
                out_l[rows] = (own[rows] + suf[rows].astype(F32)).astype(BF16)
                left(q).start()

        return 0

    lax.fori_loop(0, PIECES + (LINE - 1) * SKEW, step, 0)

    proj[...] = (own[...] + (pre[...].astype(F32) + suf[...].astype(F32))).astype(BF16)

    btf[448:, :] = jnp.zeros((8, RANK), F32)

    def swap_terms(x):
        return pltpu.make_async_remote_copy(
            btb.at[1 - core, pl.ds(x * 8, 8)], cbuf.at[pl.ds(x * 8, 8)], t_send.at[x], t_recv.at[x],
            device_id=other_core, device_id_type=MESH)

    def terms(i, _):
        x = lax.rem(xx + 1 + i, 4)
        first = pl.multiple_of(x * 448, 448)
        btf[0:448, :] = jnp.dot(got[pl.ds(first, 448), :], proj[...], preferred_element_type=F32)
        for k in range(8):
            two = btf[56 * k : 56 * k + 64, :]
            j = x * 8 + (k % 4) * 2 + k // 4
            btb[0, j] = two[:PAD].astype(BF16)
            btb[1, j] = pltpu.roll(two, 64 - OWNED, 0)[:PAD].astype(BF16)
        swap_terms(x).start()
        return 0

    lax.fori_loop(0, 4, terms, 0)

    def send_terms(q):
        return pltpu.make_async_remote_copy(
            s1.at[pl.ds(q * 2, 2)], rb.at[pos], b_send.at[q], b_recv.at[pos], device_id=at_pos(q), device_id_type=MESH)

    def add_cores(i, _):
        x = lax.rem(xx + 1 + i, 4)
        swap_terms(x).wait()
        for k in range(4):
            q = x * 4 + lax.rem(y + 1 + k, 4)
            both = pl.ds(q * 2, 2)
            s1[both] = (btb[core, both].astype(F32) + cbuf[both].astype(F32)).astype(BF16)

            @pl.when(q != pos)
            def _():
                send_terms(q).start()

        return 0

    lax.fori_loop(0, 4, add_cores, 0)

    def add_terms(i, acc):
        q = lax.rem(pos + 16 - i, 16)
        pltpu.make_async_remote_copy(
            s1.at[pl.ds(q * 2, 2)], rb.at[q], b_send.at[q], b_recv.at[q],
            device_id=at_pos(q), device_id_type=MESH).wait_recv()
        return (acc[0] + rb[q, zh].astype(F32), acc[1] + rb[q, 1 - zh].astype(F32))

    mine, theirs = lax.fori_loop(
        1, 16, add_terms, (s1[2 * pos + zh].astype(F32), s1[2 * pos + 1 - zh].astype(F32)))
    zsend[...] = theirs.astype(BF16)
    swap_sum = pltpu.make_async_remote_copy(
        zsend, zrecv, z_send.at[1], z_recv.at[1], device_id=other_zh, device_id_type=MESH)
    swap_sum.start()
    swap_sum.wait()
    grad_sub = to_natural(mine + zrecv[...].astype(F32))[:OWNED]

    moment_new, second_new, direction = adam_direction(grad_sub, mom[...], sec[...])
    mnew[...] = moment_new
    snew[...] = second_new
    direct[OWNED - 4 :, :] = jnp.zeros((PAD - OWNED + 4, RANK), F32)
    direct[:OWNED, :] = to_halves(direction)
    dirs[f] = direct[...].astype(BF16)

    def send_dir(i):
        return pltpu.make_async_remote_copy(
            dirs.at[f], dirs.at[f], d_send.at[i], d_recv.at[f],
            device_id=(d, lax.rem(f + i, LINE)), device_id_type=MESH)

    def each_line(action):
        def body(i, _):
            action(i)
            return 0
        lax.fori_loop(1, LINE, body, 0)

    each_line(lambda i: send_dir(i).start())

    def wait_dir(i):
        q = lax.rem(f + LINE - i, LINE)
        pltpu.make_async_remote_copy(
            dirs.at[q], dirs.at[q], d_send.at[i], d_recv.at[q], device_id=(d, q), device_id_type=MESH).wait_recv()

    each_line(wait_dir)
    both = basis[...].reshape(RANK, FEATURES)
    upd[...] = jnp.dot(
        dirs[...].reshape(LINE * PAD, RANK), both, preferred_element_type=F32).astype(BF16)

    each_peer(lambda i: send_terms(lax.rem(pos + i, 16)).wait_send())
    each_line(lambda i: send_dir(i).wait_send())

    def sent(p, _):
        @pl.when(f < LINE - 1)
        def _():
            right(p).wait_send()

        @pl.when(f > 0)
        def _():
            left(p).wait_send()

        return 0

    lax.fori_loop(0, PIECES, sent, 0)


def local(inputs, grad_out, projector, moment, second):
    blk = projector.T.reshape(4, 8, 128).transpose(1, 0, 2).reshape(32, 128)
    vmem = pl.BlockSpec(memory_space=pltpu.VMEM)
    anywhere = pl.BlockSpec(memory_space=pl.ANY)
    dma = pltpu.SemaphoreType.DMA
    update, moment_new, second_new = pl.pallas_call(
        kernel,
        out_shape=(
            jax.ShapeDtypeStruct((LINE * PAD, FEATURES), BF16),
            jax.ShapeDtypeStruct((OWNED, RANK), F32),
            jax.ShapeDtypeStruct((OWNED, RANK), F32),
        ),
        in_specs=[vmem, anywhere, anywhere, anywhere, anywhere],
        out_specs=(vmem, vmem, vmem),
        scratch_shapes=[
            pltpu.VMEM((TOKENS, FEATURES), BF16),
            pltpu.VMEM((TOKENS, UNITS), BF16),
            pltpu.VMEM((OWNED, RANK), F32),
            pltpu.VMEM((OWNED, RANK), F32),
            pltpu.VMEM((UNITS, TOKENS), BF16),
            pltpu.VMEM((2, 2, 16, 32, 128), BF16),
            pltpu.VMEM((2, 128, FEATURES), BF16),
            pltpu.VMEM((TOKENS, RANK), F32),
            pltpu.VMEM((TOKENS, RANK), BF16),
            pltpu.VMEM((TOKENS, RANK), BF16),
            pltpu.VMEM((TOKENS, RANK), BF16),
            pltpu.VMEM((TOKENS, RANK), BF16),
            pltpu.VMEM((TOKENS, RANK), BF16),
            pltpu.VMEM((456, RANK), F32),
            pltpu.VMEM((2, 32, PAD, RANK), BF16),
            pltpu.VMEM((32, PAD, RANK), BF16),
            pltpu.VMEM((32, PAD, RANK), BF16),
            pltpu.VMEM((16, 2, PAD, RANK), BF16),
            pltpu.VMEM((PAD, RANK), BF16),
            pltpu.VMEM((PAD, RANK), BF16),
            pltpu.VMEM((PAD, RANK), F32),
            pltpu.VMEM((LINE, PAD, RANK), BF16),
            dma((4,)),
            dma((2,)), dma((2,)),
            dma((2, 16)), dma((2, 16)),
            dma((2,)), dma((2,)),
            dma((PIECES,)), dma((PIECES,)), dma((PIECES,)), dma((PIECES,)),
            dma((16,)), dma((16,)),
            dma((LINE,)), dma((LINE,)),
            dma((4,)), dma((4,)),
        ],
        compiler_params=pltpu.CompilerParams(
            collective_id=0, has_side_effects=True, vmem_limit_bytes=48 * 1024 * 1024),
    )(*[pltpu.with_memory_space_constraint(v, pltpu.HBM) for v in (blk, inputs, grad_out, moment, second)])
    return (update.reshape(LINE, PAD, FEATURES)[:, :OWNED], moment_new, second_new)


def solution(mesh):
    return jax.shard_map(
        local,
        mesh=mesh,
        in_specs=(
            P("dp", "fsdp"),
            P("dp", "fsdp"),
            P("fsdp", "dp"),
            P(("fsdp", "dp"), None),
            P(("fsdp", "dp"), None),
        ),
        out_specs=(P(None, "dp", "fsdp"), P(("fsdp", "dp"), None), P(("fsdp", "dp"), None)),
        check_vma=False,
    )
```

```python
import functools

import jax
import jax.numpy as jnp
from jax import lax
from jax.experimental import pallas as pl
from jax.experimental.pallas import tpu as pltpu
from jax.sharding import PartitionSpec as P

MESH = pl.DeviceIdType.MESH
F32 = jnp.float32
BF16 = jnp.bfloat16

STEP = 10
BETA_FIRST = 0.9
BETA_SECOND = 0.999
EPSILON = 1e-08

TOKENS = 768
FEATURES = 1024
UNITS = 1792
RANK = 256
OWNED = 28
PAD = 32
LINE = 8
PIECE = 64
PIECES = TOKENS // PIECE
SKEW = 9
GATHERED = 12
PROJECTED = 17
LATER = 24
ADDED = 5


def adam_direction(grad_sub, moment, second):
    moment_new = BETA_FIRST * moment + (1.0 - BETA_FIRST) * grad_sub
    second_new = BETA_SECOND * second + (1.0 - BETA_SECOND) * grad_sub * grad_sub
    first_hat = moment_new / (1.0 - BETA_FIRST**STEP)
    second_hat = second_new / (1.0 - BETA_SECOND**STEP)
    direction = first_hat / (jnp.sqrt(second_hat) + EPSILON)
    return (moment_new, second_new, direction)


def to_natural(v):
    return jnp.concatenate([v[:, zh * 128 + x * 32 : zh * 128 + x * 32 + 32] for x in range(4) for zh in range(2)], axis=1)


def to_halves(v):
    return jnp.concatenate([v[:, x * 64 + zh * 32 : x * 64 + zh * 32 + 32] for zh in range(2) for x in range(4)], axis=1)


def kernel(
    blk, x_hbm, go_hbm, mom_hbm, sec_hbm,
    upd, mnew, snew,
    x_v, go_v, mom, sec, got, raw, basis, own, pre, suf, out_r, out_l, proj, btf, btb, cbuf, s1, rb, zsend, zrecv, total, direct, dirs,
    load_sem, z_send, z_recv, g_send, g_recv, c_send, c_recv, r_send, r_recv, l_send, l_recv, b_send, b_recv, d_send, d_recv, t_send, t_recv,
):
    d = lax.axis_index("dp")
    f = lax.axis_index("fsdp")
    core = lax.rem(d, 2)
    y = lax.rem(d // 2, 4)
    zh = lax.rem(d // 8, 2)
    xx = d // 16
    pos = xx * 4 + y
    other_core = (d + 1 - 2 * core, f)
    other_zh = (d + 8 - 16 * zh, f)

    def at_pos(q):
        return (((q // 4) * 2 + zh) * 8 + lax.rem(q, 4) * 2 + core, f)

    load_x = pltpu.make_async_copy(x_hbm, x_v, load_sem.at[0])
    load_go = pltpu.make_async_copy(go_hbm, go_v, load_sem.at[1])
    load_mom = pltpu.make_async_copy(mom_hbm, mom, load_sem.at[2])
    load_sec = pltpu.make_async_copy(sec_hbm, sec, load_sem.at[3])
    load_go.start()
    load_x.start()
    load_mom.start()
    load_sec.start()

    barrier = pltpu.get_barrier_semaphore()
    pl.semaphore_signal(barrier, inc=1, device_id=other_zh, device_id_type=MESH)
    pl.semaphore_signal(barrier, inc=1, device_id=other_core, device_id_type=MESH)

    def greet(i, _):
        pl.semaphore_signal(barrier, inc=1, device_id=at_pos(lax.rem(pos + i, 16)), device_id_type=MESH)
        return 0

    lax.fori_loop(1, 16, greet, 0)

    def greet_line(i, _):
        pl.semaphore_signal(barrier, inc=1, device_id=(d, lax.rem(f + i, LINE)), device_id_type=MESH)
        return 0

    lax.fori_loop(1, LINE, greet_line, 0)
    raw[zh, core, pos] = blk[...]
    load_go.wait()

    def turn(i, _):
        cols = pl.ds(pl.multiple_of(i * 128, 128), 128)
        got[cols, :] = go_v[:, cols].T
        return 0

    lax.fori_loop(0, UNITS // 128, turn, 0)

    @pl.when(f == 0)
    def _():
        pre[:] = jnp.zeros_like(pre)

    @pl.when(f == LINE - 1)
    def _():
        suf[:] = jnp.zeros_like(suf)

    load_x.wait()
    load_mom.wait()
    load_sec.wait()
    pl.semaphore_wait(barrier, 24)

    def send_block(which, i):
        q = lax.rem(pos + i, 16)
        return pltpu.make_async_remote_copy(
            raw.at[which, core, pos], raw.at[which, core, pos], g_send.at[which, i], g_recv.at[which, pos],
            device_id=at_pos(q), device_id_type=MESH)

    def wait_block(which, i):
        q = lax.rem(pos + 16 - i, 16)
        pltpu.make_async_remote_copy(
            raw.at[which, core, q], raw.at[which, core, q], g_send.at[which, i], g_recv.at[which, q],
            device_id=at_pos(q), device_id_type=MESH).wait_recv()

    def each_peer(action):
        def body(i, _):
            action(i)
            return 0
        lax.fori_loop(1, 16, body, 0)

    swap_zh = pltpu.make_async_remote_copy(
        raw.at[zh, core, pos], raw.at[zh, core, pos], z_send.at[0], z_recv.at[0], device_id=other_zh, device_id_type=MESH)
    swap_zh.start()
    each_peer(lambda i: send_block(zh, i).start())

    def swap_core(which):
        return pltpu.make_async_remote_copy(
            raw.at[which, core], raw.at[which, core], c_send.at[which], c_recv.at[which],
            device_id=other_core, device_id_type=MESH)

    each_peer(lambda i: wait_block(zh, i))
    swap_core(zh).start()
    swap_zh.wait_recv()
    each_peer(lambda i: send_block(1 - zh, i).start())

    row = lax.broadcasted_iota(jnp.int32, (256, 256), 0)
    col = lax.broadcasted_iota(jnp.int32, (256, 256), 1)
    source = ((row // 4) % 2) * 128 + ((row // 8) % 4) * 32 + (row // 32) * 4 + row % 4
    perm = jnp.where(col == source, 1.0, 0.0).astype(BF16)

    def unfold(which):
        for x in range(4):
            blocks = jnp.concatenate(
                [raw[which, 0, 4 * x : 4 * x + 4].reshape(128, 128), raw[which, 1, 4 * x : 4 * x + 4].reshape(128, 128)], axis=0)
            placed = jnp.dot(perm, blocks, preferred_element_type=F32).astype(BF16)
            for b in range(8):
                basis[which, 32 * x : 32 * x + 32, 128 * b : 128 * b + 128] = placed[32 * b : 32 * b + 32]

    def project(which):
        own[which] = lax.dot_general(
            x_v[...], basis[which], (((1,), (1,)), ((), ())), preferred_element_type=F32)

    swap_core(zh).wait()
    unfold(zh)
    project(zh)

    def right(which, p):
        rows = pl.ds(pl.multiple_of(p * PIECE, PIECE), PIECE)
        return pltpu.make_async_remote_copy(
            out_r.at[which, rows], pre.at[which, rows], r_send.at[which, p], r_recv.at[which, p],
            device_id=(d, lax.rem(f + 1, LINE)), device_id_type=MESH)

    def left(which, p):
        rows = pl.ds(pl.multiple_of(p * PIECE, PIECE), PIECE)
        return pltpu.make_async_remote_copy(
            out_l.at[which, rows], suf.at[which, rows], l_send.at[which, p], l_recv.at[which, p],
            device_id=(d, lax.rem(f + LINE - 1, LINE)), device_id_type=MESH)

    def chain(which, t):
        p = t - f * SKEW

        @pl.when((p >= 0) & (p < PIECES))
        def _():
            @pl.when(f > 0)
            def _():
                right(which, p).wait_recv()

            @pl.when(f < LINE - 1)
            def _():
                rows = pl.ds(pl.multiple_of(p * PIECE, PIECE), PIECE)
                out_r[which, rows] = (own[which, rows] + pre[which, rows].astype(F32)).astype(BF16)
                right(which, p).start()

        q = t - (LINE - 1 - f) * SKEW

        @pl.when((q >= 0) & (q < PIECES))
        def _():
            @pl.when(f < LINE - 1)
            def _():
                left(which, q).wait_recv()

            @pl.when(f > 0)
            def _():
                rows = pl.ds(pl.multiple_of(q * PIECE, PIECE), PIECE)
                out_l[which, rows] = (own[which, rows] + suf[which, rows].astype(F32)).astype(BF16)
                left(which, q).start()

    btf[448:, :] = jnp.zeros((8, 128), F32)

    def swap_terms(which, x):
        return pltpu.make_async_remote_copy(
            btb.at[which, 1 - core, pl.ds(x * 8, 8)], cbuf.at[which, pl.ds(x * 8, 8)], t_send.at[which, x], t_recv.at[which, x],
            device_id=other_core, device_id_type=MESH)

    def make_terms(which):
        proj[...] = (own[which] + (pre[which].astype(F32) + suf[which].astype(F32))).astype(BF16)

        def terms(i, _):
            x = lax.rem(xx + 1 + i, 4)
            first = pl.multiple_of(x * 448, 448)
            btf[0:448, :] = jnp.dot(got[pl.ds(first, 448), :], proj[...], preferred_element_type=F32)
            for k in range(8):
                two = btf[56 * k : 56 * k + 64, :]
                j = x * 8 + (k % 4) * 2 + k // 4
                btb[which, 0, j] = two[:PAD].astype(BF16)
                btb[which, 1, j] = pltpu.roll(two, 64 - OWNED, 0)[:PAD].astype(BF16)
            swap_terms(which, x).start()
            return 0

        lax.fori_loop(0, 4, terms, 0)

    def send_terms(which, q):
        return pltpu.make_async_remote_copy(
            s1.at[which, pl.ds(q * 2, 2)], rb.at[which, pos], b_send.at[which, q], b_recv.at[which, pos],
            device_id=at_pos(q), device_id_type=MESH)

    def add_cores(which):
        def body(i, _):
            x = lax.rem(xx + 1 + i, 4)
            swap_terms(which, x).wait()
            for k in range(4):
                q = x * 4 + lax.rem(y + 1 + k, 4)
                both = pl.ds(q * 2, 2)
                s1[which, both] = (btb[which, core, both].astype(F32) + cbuf[which, both].astype(F32)).astype(BF16)

                @pl.when(q != pos)
                def _():
                    send_terms(which, q).start()

            return 0

        lax.fori_loop(0, 4, body, 0)

    far = jnp.maximum(f, LINE - 1 - f)
    first_done = far * SKEW + PIECES + jnp.maximum(5 - far, 0) * (LATER + 1)

    def step(t, _):
        chain(zh, t)
        chain(1 - zh, t - LATER)

        @pl.when(t == GATHERED)
        def _():
            each_peer(lambda i: wait_block(1 - zh, i))
            swap_core(1 - zh).start()

        @pl.when(t == PROJECTED)
        def _():
            swap_core(1 - zh).wait()
            unfold(1 - zh)
            project(1 - zh)

        @pl.when(t == first_done)
        def _():
            make_terms(zh)

        @pl.when(t == first_done + ADDED)
        def _():
            add_cores(zh)

        return 0

    lax.fori_loop(0, LATER + (LINE - 1) * SKEW + PIECES, step, 0)
    make_terms(1 - zh)
    add_cores(1 - zh)

    def swap_sum(which):
        return pltpu.make_async_remote_copy(
            zsend.at[which], zrecv.at[which], z_send.at[1 + which], z_recv.at[1 + which],
            device_id=other_zh, device_id_type=MESH)

    def add_chips(which):
        def body(i, acc):
            q = lax.rem(pos + 16 - i, 16)
            pltpu.make_async_remote_copy(
                s1.at[which, pl.ds(q * 2, 2)], rb.at[which, q], b_send.at[which, q], b_recv.at[which, q],
                device_id=at_pos(q), device_id_type=MESH).wait_recv()
            return (acc[0] + rb[which, q, zh].astype(F32), acc[1] + rb[which, q, 1 - zh].astype(F32))

        mine, theirs = lax.fori_loop(
            1, 16, body, (s1[which, 2 * pos + zh].astype(F32), s1[which, 2 * pos + 1 - zh].astype(F32)))
        zsend[which] = theirs.astype(BF16)
        swap_sum(which).start()
        total[which] = mine

    add_chips(zh)
    add_chips(1 - zh)
    swap_sum(zh).wait()
    swap_sum(1 - zh).wait()
    grad_sub = to_natural(jnp.concatenate([total[h] + zrecv[h].astype(F32) for h in range(2)], axis=1))[:OWNED]

    moment_new, second_new, direction = adam_direction(grad_sub, mom[...], sec[...])
    mnew[...] = moment_new
    snew[...] = second_new
    direct[OWNED - 4 :, :] = jnp.zeros((PAD - OWNED + 4, RANK), F32)
    direct[:OWNED, :] = to_halves(direction)
    dirs[f] = direct[...].astype(BF16)

    def send_dir(i):
        return pltpu.make_async_remote_copy(
            dirs.at[f], dirs.at[f], d_send.at[i], d_recv.at[f],
            device_id=(d, lax.rem(f + i, LINE)), device_id_type=MESH)

    def each_line(action):
        def body(i, _):
            action(i)
            return 0
        lax.fori_loop(1, LINE, body, 0)

    each_line(lambda i: send_dir(i).start())

    def wait_dir(i):
        q = lax.rem(f + LINE - i, LINE)
        pltpu.make_async_remote_copy(
            dirs.at[q], dirs.at[q], d_send.at[i], d_recv.at[q], device_id=(d, q), device_id_type=MESH).wait_recv()

    each_line(wait_dir)
    both = basis[...].reshape(RANK, FEATURES)
    upd[...] = jnp.dot(
        dirs[...].reshape(LINE * PAD, RANK), both, preferred_element_type=F32).astype(BF16)

    swap_zh.wait_send()
    each_line(lambda i: send_dir(i).wait_send())
    for which in range(2):
        each_peer(lambda i: send_block(which, i).wait_send())
        each_peer(lambda i: send_terms(which, lax.rem(pos + i, 16)).wait_send())

        def sent(p, _):
            @pl.when(f < LINE - 1)
            def _():
                right(which, p).wait_send()

            @pl.when(f > 0)
            def _():
                left(which, p).wait_send()

            return 0

        lax.fori_loop(0, PIECES, sent, 0)


def local(inputs, grad_out, projector, moment, second):
    blk = projector.T.reshape(4, 8, 128).transpose(1, 0, 2).reshape(32, 128)
    vmem = pl.BlockSpec(memory_space=pltpu.VMEM)
    anywhere = pl.BlockSpec(memory_space=pl.ANY)
    dma = pltpu.SemaphoreType.DMA
    update, moment_new, second_new = pl.pallas_call(
        kernel,
        out_shape=(
            jax.ShapeDtypeStruct((LINE * PAD, FEATURES), BF16),
            jax.ShapeDtypeStruct((OWNED, RANK), F32),
            jax.ShapeDtypeStruct((OWNED, RANK), F32),
        ),
        in_specs=[vmem, anywhere, anywhere, anywhere, anywhere],
        out_specs=(vmem, vmem, vmem),
        scratch_shapes=[
            pltpu.VMEM((TOKENS, FEATURES), BF16),
            pltpu.VMEM((TOKENS, UNITS), BF16),
            pltpu.VMEM((OWNED, RANK), F32),
            pltpu.VMEM((OWNED, RANK), F32),
            pltpu.VMEM((UNITS, TOKENS), BF16),
            pltpu.VMEM((2, 2, 16, 32, 128), BF16),
            pltpu.VMEM((2, 128, FEATURES), BF16),
            pltpu.VMEM((2, TOKENS, 128), F32),
            pltpu.VMEM((2, TOKENS, 128), BF16),
            pltpu.VMEM((2, TOKENS, 128), BF16),
            pltpu.VMEM((2, TOKENS, 128), BF16),
            pltpu.VMEM((2, TOKENS, 128), BF16),
            pltpu.VMEM((TOKENS, 128), BF16),
            pltpu.VMEM((456, 128), F32),
            pltpu.VMEM((2, 2, 32, PAD, 128), BF16),
            pltpu.VMEM((2, 32, PAD, 128), BF16),
            pltpu.VMEM((2, 32, PAD, 128), BF16),
            pltpu.VMEM((2, 16, 2, PAD, 128), BF16),
            pltpu.VMEM((2, PAD, 128), BF16),
            pltpu.VMEM((2, PAD, 128), BF16),
            pltpu.VMEM((2, PAD, 128), F32),
            pltpu.VMEM((PAD, RANK), F32),
            pltpu.VMEM((LINE, PAD, RANK), BF16),
            dma((4,)),
            dma((3,)), dma((3,)),
            dma((2, 16)), dma((2, 16)),
            dma((2,)), dma((2,)),
            dma((2, PIECES)), dma((2, PIECES)), dma((2, PIECES)), dma((2, PIECES)),
            dma((2, 16)), dma((2, 16)),
            dma((LINE,)), dma((LINE,)),
            dma((2, 4)), dma((2, 4)),
        ],
        compiler_params=pltpu.CompilerParams(
            collective_id=0, has_side_effects=True, vmem_limit_bytes=48 * 1024 * 1024),
    )(*[pltpu.with_memory_space_constraint(v, pltpu.HBM) for v in (blk, inputs, grad_out, moment, second)])
    return (update.reshape(LINE, PAD, FEATURES)[:, :OWNED], moment_new, second_new)


def solution(mesh):
    return jax.shard_map(
        local,
        mesh=mesh,
        in_specs=(
            P("dp", "fsdp"),
            P("dp", "fsdp"),
            P("fsdp", "dp"),
            P(("fsdp", "dp"), None),
            P(("fsdp", "dp"), None),
        ),
        out_specs=(P(None, "dp", "fsdp"), P(("fsdp", "dp"), None), P(("fsdp", "dp"), None)),
        check_vma=False,
    )
```

```python
import functools

import jax
import jax.numpy as jnp
from jax import lax
from jax.experimental import pallas as pl
from jax.experimental.pallas import tpu as pltpu
from jax.sharding import PartitionSpec as P

MESH = pl.DeviceIdType.MESH
F32 = jnp.float32
BF16 = jnp.bfloat16

STEP = 10
BETA_FIRST = 0.9
BETA_SECOND = 0.999
EPSILON = 1e-08

TOKENS = 768
FEATURES = 1024
UNITS = 1792
RANK = 256
OWNED = 28
PAD = 32
LINE = 8
PAIRS = LINE // 2
SHARE = TOKENS // 2
PIECE = 64
PIECES = SHARE // PIECE
MERGED = 5
SKEW = 6
GATHERED = 8
PROJECTED = 11
LATER = 15
ADDED = 4


def adam_direction(grad_sub, moment, second):
    moment_new = BETA_FIRST * moment + (1.0 - BETA_FIRST) * grad_sub
    second_new = BETA_SECOND * second + (1.0 - BETA_SECOND) * grad_sub * grad_sub
    first_hat = moment_new / (1.0 - BETA_FIRST**STEP)
    second_hat = second_new / (1.0 - BETA_SECOND**STEP)
    direction = first_hat / (jnp.sqrt(second_hat) + EPSILON)
    return (moment_new, second_new, direction)


def to_natural(v):
    return jnp.concatenate([v[:, zh * 128 + x * 32 : zh * 128 + x * 32 + 32] for x in range(4) for zh in range(2)], axis=1)


def to_halves(v):
    return jnp.concatenate([v[:, x * 64 + zh * 32 : x * 64 + zh * 32 + 32] for zh in range(2) for x in range(4)], axis=1)


def kernel(
    blk, x_hbm, go_hbm, mom_hbm, sec_hbm,
    upd, mnew, snew,
    x_v, go_v, mom, sec, got, raw, basis, own, out_p, pair_in, pre, suf, out_r, out_l, proj, btf, btb, cbuf, s1, rb, zsend, zrecv, total, direct, dirs,
    load_sem, z_send, z_recv, g_send, g_recv, c_send, c_recv, r_send, r_recv, l_send, l_recv, b_send, b_recv, d_send, d_recv, t_send, t_recv,
    p_send, p_recv, q_send, q_recv,
):
    d = lax.axis_index("dp")
    f = lax.axis_index("fsdp")
    core = lax.rem(d, 2)
    y = lax.rem(d // 2, 4)
    zh = lax.rem(d // 8, 2)
    xx = d // 16
    pos = xx * 4 + y
    pair = f // 2
    side = lax.rem(f, 2)
    other_side = (d, f + 1 - 2 * side)
    other_core = (d + 1 - 2 * core, f)
    other_zh = (d + 8 - 16 * zh, f)

    def at_pos(q):
        return (((q // 4) * 2 + zh) * 8 + lax.rem(q, 4) * 2 + core, f)

    load_x = pltpu.make_async_copy(x_hbm, x_v, load_sem.at[0])
    load_go = pltpu.make_async_copy(go_hbm, go_v, load_sem.at[1])
    load_mom = pltpu.make_async_copy(mom_hbm, mom, load_sem.at[2])
    load_sec = pltpu.make_async_copy(sec_hbm, sec, load_sem.at[3])
    load_go.start()
    load_x.start()
    load_mom.start()
    load_sec.start()

    barrier = pltpu.get_barrier_semaphore()
    pl.semaphore_signal(barrier, inc=1, device_id=other_zh, device_id_type=MESH)
    pl.semaphore_signal(barrier, inc=1, device_id=other_core, device_id_type=MESH)

    def greet(i, _):
        pl.semaphore_signal(barrier, inc=1, device_id=at_pos(lax.rem(pos + i, 16)), device_id_type=MESH)
        return 0

    lax.fori_loop(1, 16, greet, 0)

    def greet_line(i, _):
        pl.semaphore_signal(barrier, inc=1, device_id=(d, lax.rem(f + i, LINE)), device_id_type=MESH)
        return 0

    lax.fori_loop(1, LINE, greet_line, 0)
    raw[zh, core, pos] = blk[...]
    load_go.wait()

    def turn(i, _):
        cols = pl.ds(pl.multiple_of(i * 128, 128), 128)
        got[cols, :] = go_v[:, cols].T
        return 0

    lax.fori_loop(0, UNITS // 128, turn, 0)

    @pl.when(pair == 0)
    def _():
        pre[:] = jnp.zeros_like(pre)

    @pl.when(pair == PAIRS - 1)
    def _():
        suf[:] = jnp.zeros_like(suf)

    load_x.wait()
    load_mom.wait()
    load_sec.wait()
    pl.semaphore_wait(barrier, 24)

    def send_block(which, i):
        q = lax.rem(pos + i, 16)
        return pltpu.make_async_remote_copy(
            raw.at[which, core, pos], raw.at[which, core, pos], g_send.at[which, i], g_recv.at[which, pos],
            device_id=at_pos(q), device_id_type=MESH)

    def wait_block(which, i):
        q = lax.rem(pos + 16 - i, 16)
        pltpu.make_async_remote_copy(
            raw.at[which, core, q], raw.at[which, core, q], g_send.at[which, i], g_recv.at[which, q],
            device_id=at_pos(q), device_id_type=MESH).wait_recv()

    def each_peer(action):
        def body(i, _):
            action(i)
            return 0
        lax.fori_loop(1, 16, body, 0)

    swap_zh = pltpu.make_async_remote_copy(
        raw.at[zh, core, pos], raw.at[zh, core, pos], z_send.at[0], z_recv.at[0], device_id=other_zh, device_id_type=MESH)
    swap_zh.start()
    each_peer(lambda i: send_block(zh, i).start())

    def swap_core(which):
        return pltpu.make_async_remote_copy(
            raw.at[which, core], raw.at[which, core], c_send.at[which], c_recv.at[which],
            device_id=other_core, device_id_type=MESH)

    each_peer(lambda i: wait_block(zh, i))
    swap_core(zh).start()
    swap_zh.wait_recv()
    each_peer(lambda i: send_block(1 - zh, i).start())

    row = lax.broadcasted_iota(jnp.int32, (256, 256), 0)
    col = lax.broadcasted_iota(jnp.int32, (256, 256), 1)
    source = ((row // 4) % 2) * 128 + ((row // 8) % 4) * 32 + (row // 32) * 4 + row % 4
    perm = jnp.where(col == source, 1.0, 0.0).astype(BF16)

    def unfold(which):
        for x in range(4):
            blocks = jnp.concatenate(
                [raw[which, 0, 4 * x : 4 * x + 4].reshape(128, 128), raw[which, 1, 4 * x : 4 * x + 4].reshape(128, 128)], axis=0)
            placed = jnp.dot(perm, blocks, preferred_element_type=F32).astype(BF16)
            for b in range(8):
                basis[which, 32 * x : 32 * x + 32, 128 * b : 128 * b + 128] = placed[32 * b : 32 * b + 32]

    def project(which):
        own[which] = lax.dot_general(
            x_v[...], basis[which], (((1,), (1,)), ((), ())), preferred_element_type=F32)

    swap_core(zh).wait()
    unfold(zh)
    project(zh)

    def mine_at(p):
        return pl.ds(pl.multiple_of(side * SHARE + p * PIECE, PIECE), PIECE)

    def give(which, p):
        rows = pl.ds(pl.multiple_of(p * PIECE, PIECE), PIECE)
        return pltpu.make_async_remote_copy(
            out_p.at[which, rows], pair_in.at[which, rows], p_send.at[which, p], p_recv.at[which, p],
            device_id=other_side, device_id_type=MESH)

    def right(which, p):
        rows = pl.ds(pl.multiple_of(p * PIECE, PIECE), PIECE)
        return pltpu.make_async_remote_copy(
            out_r.at[which, rows], pre.at[which, rows], r_send.at[which, p], r_recv.at[which, p],
            device_id=(d, lax.rem(f + 2, LINE)), device_id_type=MESH)

    def left(which, p):
        rows = pl.ds(pl.multiple_of(p * PIECE, PIECE), PIECE)
        return pltpu.make_async_remote_copy(
            out_l.at[which, rows], suf.at[which, rows], l_send.at[which, p], l_recv.at[which, p],
            device_id=(d, lax.rem(f + LINE - 2, LINE)), device_id_type=MESH)

    def share(which, p):
        rows = mine_at(p)
        return pltpu.make_async_remote_copy(
            proj.at[which, rows], proj.at[which, rows], q_send.at[which, p], q_recv.at[which, p],
            device_id=other_side, device_id_type=MESH)

    def shared(which, p):
        rows = pl.ds(pl.multiple_of((1 - side) * SHARE + p * PIECE, PIECE), PIECE)
        return pltpu.make_async_remote_copy(
            proj.at[which, rows], proj.at[which, rows], q_send.at[which, p], q_recv.at[which, p],
            device_id=other_side, device_id_type=MESH)

    far = jnp.maximum(pair, PAIRS - 1 - pair)

    def chain(which, t):
        @pl.when((t >= 0) & (t < PIECES))
        def _():
            rows = pl.ds(pl.multiple_of(t * PIECE, PIECE), PIECE)
            theirs = pl.ds(pl.multiple_of((1 - side) * SHARE + t * PIECE, PIECE), PIECE)
            out_p[which, rows] = own[which, theirs].astype(BF16)
            give(which, t).start()

        m = t - MERGED

        @pl.when((m >= 0) & (m < PIECES))
        def _():
            give(which, m).wait_recv()
            rows = pl.ds(pl.multiple_of(m * PIECE, PIECE), PIECE)
            own[which, mine_at(m)] += pair_in[which, rows].astype(F32)

        p = m - pair * SKEW

        @pl.when((p >= 0) & (p < PIECES))
        def _():
            @pl.when(pair > 0)
            def _():
                right(which, p).wait_recv()

            @pl.when(pair < PAIRS - 1)
            def _():
                rows = pl.ds(pl.multiple_of(p * PIECE, PIECE), PIECE)
                out_r[which, rows] = (own[which, mine_at(p)] + pre[which, rows].astype(F32)).astype(BF16)
                right(which, p).start()

        q = m - (PAIRS - 1 - pair) * SKEW

        @pl.when((q >= 0) & (q < PIECES))
        def _():
            @pl.when(pair < PAIRS - 1)
            def _():
                left(which, q).wait_recv()

            @pl.when(pair > 0)
            def _():
                rows = pl.ds(pl.multiple_of(q * PIECE, PIECE), PIECE)
                out_l[which, rows] = (own[which, mine_at(q)] + suf[which, rows].astype(F32)).astype(BF16)
                left(which, q).start()

        e = m - far * SKEW

        @pl.when((e >= 0) & (e < PIECES))
        def _():
            rows = pl.ds(pl.multiple_of(e * PIECE, PIECE), PIECE)
            proj[which, mine_at(e)] = (
                own[which, mine_at(e)] + (pre[which, rows].astype(F32) + suf[which, rows].astype(F32))).astype(BF16)
            share(which, e).start()

    btf[224:, :] = jnp.zeros((8, 128), F32)

    def swap_terms(which, z, x):
        rows = pl.ds(x * 4, 4)
        return pltpu.make_async_remote_copy(
            btb.at[which, 1 - core, z, rows], cbuf.at[which, z, rows], t_send.at[which, z, x], t_recv.at[which, z, x],
            device_id=other_core, device_id_type=MESH)

    def turn_of(i):
        return (lax.rem(1 - zh + i // 4, 2), lax.rem(xx + 1 + i, 4))

    def make_terms(which):
        def arrived(p, _):
            shared(which, p).wait_recv()
            return 0

        lax.fori_loop(0, PIECES, arrived, 0)

        def terms(i, _):
            z, x = turn_of(i)
            first = pl.multiple_of(x * 448 + z * 224, 32)
            btf[0:224, :] = jnp.dot(got[pl.ds(first, 224), :], proj[which], preferred_element_type=F32)
            for k in range(4):
                two = btf[56 * k : 56 * k + 64, :]
                btb[which, 0, z, x * 4 + k] = two[:PAD].astype(BF16)
                btb[which, 1, z, x * 4 + k] = pltpu.roll(two, 64 - OWNED, 0)[:PAD].astype(BF16)
            swap_terms(which, z, x).start()
            return 0

        lax.fori_loop(0, 8, terms, 0)

    def send_terms(which, z, q):
        return pltpu.make_async_remote_copy(
            s1.at[which, z, q], rb.at[which, z, pos], b_send.at[which, z, q], b_recv.at[which, z, pos],
            device_id=at_pos(q), device_id_type=MESH)

    def add_cores(which):
        def body(i, _):
            z, x = turn_of(i)
            swap_terms(which, z, x).wait()
            for k in range(4):
                q = x * 4 + lax.rem(y + 1 + k, 4)
                s1[which, z, q] = (btb[which, core, z, q].astype(F32) + cbuf[which, z, q].astype(F32)).astype(BF16)

                @pl.when(q != pos)
                def _():
                    send_terms(which, z, q).start()

            return 0

        lax.fori_loop(0, 8, body, 0)

    first_done = MERGED + far * SKEW + PIECES + (far - 2) * MERGED + (3 - far) * (LATER + 1)

    def step(t, _):
        chain(zh, t)
        chain(1 - zh, t - LATER)

        @pl.when(t == GATHERED)
        def _():
            each_peer(lambda i: wait_block(1 - zh, i))
            swap_core(1 - zh).start()

        @pl.when(t == PROJECTED)
        def _():
            swap_core(1 - zh).wait()
            unfold(1 - zh)
            project(1 - zh)

        @pl.when(t == first_done)
        def _():
            make_terms(zh)

        @pl.when(t == first_done + ADDED)
        def _():
            add_cores(zh)

        return 0

    lax.fori_loop(0, LATER + MERGED + (PAIRS - 1) * SKEW + PIECES + ADDED, step, 0)
    make_terms(1 - zh)
    add_cores(1 - zh)

    def swap_sum(which):
        return pltpu.make_async_remote_copy(
            zsend.at[which], zrecv.at[which], z_send.at[1 + which], z_recv.at[1 + which],
            device_id=other_zh, device_id_type=MESH)

    def add_chips(which, z):
        def body(i, acc):
            q = lax.rem(pos + 16 - i, 16)
            pltpu.make_async_remote_copy(
                s1.at[which, z, q], rb.at[which, z, q], b_send.at[which, z, q], b_recv.at[which, z, q],
                device_id=at_pos(q), device_id_type=MESH).wait_recv()
            return acc + rb[which, z, q].astype(F32)

        return lax.fori_loop(1, 16, body, s1[which, z, pos].astype(F32))

    for which in (zh, 1 - zh):
        zsend[which] = add_chips(which, 1 - zh).astype(BF16)
        swap_sum(which).start()

    for which in (zh, 1 - zh):
        total[which] = add_chips(which, zh)

    swap_sum(zh).wait()
    swap_sum(1 - zh).wait()
    grad_sub = to_natural(jnp.concatenate([total[h] + zrecv[h].astype(F32) for h in range(2)], axis=1))[:OWNED]

    moment_new, second_new, direction = adam_direction(grad_sub, mom[...], sec[...])
    mnew[...] = moment_new
    snew[...] = second_new
    direct[OWNED - 4 :, :] = jnp.zeros((PAD - OWNED + 4, RANK), F32)
    direct[:OWNED, :] = to_halves(direction)
    dirs[f] = direct[...].astype(BF16)

    def send_dir(i):
        return pltpu.make_async_remote_copy(
            dirs.at[f], dirs.at[f], d_send.at[i], d_recv.at[f],
            device_id=(d, lax.rem(f + i, LINE)), device_id_type=MESH)

    def each_line(action):
        def body(i, _):
            action(i)
            return 0
        lax.fori_loop(1, LINE, body, 0)

    each_line(lambda i: send_dir(i).start())

    def wait_dir(i):
        q = lax.rem(f + LINE - i, LINE)
        pltpu.make_async_remote_copy(
            dirs.at[q], dirs.at[q], d_send.at[i], d_recv.at[q], device_id=(d, q), device_id_type=MESH).wait_recv()

    each_line(wait_dir)
    both = basis[...].reshape(RANK, FEATURES)
    row = lax.broadcasted_iota(jnp.int32, (OWNED * LINE, LINE * PAD), 0)
    col = lax.broadcasted_iota(jnp.int32, (OWNED * LINE, LINE * PAD), 1)
    order = jnp.where(col == (row % LINE) * PAD + row // LINE, 1.0, 0.0).astype(BF16)
    ordered = jnp.dot(order, dirs[...].reshape(LINE * PAD, RANK), preferred_element_type=F32).astype(BF16)
    upd[...] = jnp.dot(ordered, both, preferred_element_type=F32).astype(BF16)

    swap_zh.wait_send()
    each_line(lambda i: send_dir(i).wait_send())
    for which in range(2):
        each_peer(lambda i: send_block(which, i).wait_send())
        for z in range(2):
            each_peer(lambda i: send_terms(which, z, lax.rem(pos + i, 16)).wait_send())

        def sent(p, _):
            give(which, p).wait_send()
            share(which, p).wait_send()

            @pl.when(pair < PAIRS - 1)
            def _():
                right(which, p).wait_send()

            @pl.when(pair > 0)
            def _():
                left(which, p).wait_send()

            return 0

        lax.fori_loop(0, PIECES, sent, 0)


def local(inputs, grad_out, projector, moment, second):
    blk = projector.T.reshape(4, 8, 128).transpose(1, 0, 2).reshape(32, 128)
    vmem = pl.BlockSpec(memory_space=pltpu.VMEM)
    anywhere = pl.BlockSpec(memory_space=pl.ANY)
    dma = pltpu.SemaphoreType.DMA
    update, moment_new, second_new = pl.pallas_call(
        kernel,
        out_shape=(
            jax.ShapeDtypeStruct((OWNED * LINE, FEATURES), BF16),
            jax.ShapeDtypeStruct((OWNED, RANK), F32),
            jax.ShapeDtypeStruct((OWNED, RANK), F32),
        ),
        in_specs=[vmem, anywhere, anywhere, anywhere, anywhere],
        out_specs=(vmem, vmem, vmem),
        scratch_shapes=[
            pltpu.VMEM((TOKENS, FEATURES), BF16),
            pltpu.VMEM((TOKENS, UNITS), BF16),
            pltpu.VMEM((OWNED, RANK), F32),
            pltpu.VMEM((OWNED, RANK), F32),
            pltpu.VMEM((UNITS, TOKENS), BF16),
            pltpu.VMEM((2, 2, 16, 32, 128), BF16),
            pltpu.VMEM((2, 128, FEATURES), BF16),
            pltpu.VMEM((2, TOKENS, 128), F32),
            pltpu.VMEM((2, SHARE, 128), BF16),
            pltpu.VMEM((2, SHARE, 128), BF16),
            pltpu.VMEM((2, SHARE, 128), BF16),
            pltpu.VMEM((2, SHARE, 128), BF16),
            pltpu.VMEM((2, SHARE, 128), BF16),
            pltpu.VMEM((2, SHARE, 128), BF16),
            pltpu.VMEM((2, TOKENS, 128), BF16),
            pltpu.VMEM((232, 128), F32),
            pltpu.VMEM((2, 2, 2, 16, PAD, 128), BF16),
            pltpu.VMEM((2, 2, 16, PAD, 128), BF16),
            pltpu.VMEM((2, 2, 16, PAD, 128), BF16),
            pltpu.VMEM((2, 2, 16, PAD, 128), BF16),
            pltpu.VMEM((2, PAD, 128), BF16),
            pltpu.VMEM((2, PAD, 128), BF16),
            pltpu.VMEM((2, PAD, 128), F32),
            pltpu.VMEM((PAD, RANK), F32),
            pltpu.VMEM((LINE, PAD, RANK), BF16),
            dma((4,)),
            dma((3,)), dma((3,)),
            dma((2, 16)), dma((2, 16)),
            dma((2,)), dma((2,)),
            dma((2, PIECES)), dma((2, PIECES)), dma((2, PIECES)), dma((2, PIECES)),
            dma((2, 2, 16)), dma((2, 2, 16)),
            dma((LINE,)), dma((LINE,)),
            dma((2, 2, 4)), dma((2, 2, 4)),
            dma((2, PIECES)), dma((2, PIECES)), dma((2, PIECES)), dma((2, PIECES)),
        ],
        compiler_params=pltpu.CompilerParams(
            collective_id=0, has_side_effects=True, vmem_limit_bytes=48 * 1024 * 1024),
    )(*[pltpu.with_memory_space_constraint(v, pltpu.HBM) for v in (blk, inputs, grad_out, moment, second)])
    return (update.reshape(OWNED, LINE, FEATURES).transpose(1, 0, 2), moment_new, second_new)


def solution(mesh):
    return jax.shard_map(
        local,
        mesh=mesh,
        in_specs=(
            P("dp", "fsdp"),
            P("dp", "fsdp"),
            P("fsdp", "dp"),
            P(("fsdp", "dp"), None),
            P(("fsdp", "dp"), None),
        ),
        out_specs=(P(None, "dp", "fsdp"), P(("fsdp", "dp"), None), P(("fsdp", "dp"), None)),
        check_vma=False,
    )
```

```python
import functools

import jax
import jax.numpy as jnp
from jax import lax
from jax.experimental import pallas as pl
from jax.experimental.pallas import tpu as pltpu
from jax.sharding import PartitionSpec as P

MESH = pl.DeviceIdType.MESH
F32 = jnp.float32
BF16 = jnp.bfloat16

STEP = 10
BETA_FIRST = 0.9
BETA_SECOND = 0.999
EPSILON = 1e-08

TOKENS = 768
FEATURES = 1024
UNITS = 1792
RANK = 256
OWNED = 28
PAD = 32
LINE = 8
PAIRS = LINE // 2
SHARE = TOKENS // 2
PIECE = 128
PIECES = SHARE // PIECE
MERGED = 3
SKEW = 4
GATHERED = 4
PROJECTED = 5
LATER = 7
ADDED = 4
BEHIND = 3


def adam_direction(grad_sub, moment, second):
    moment_new = BETA_FIRST * moment + (1.0 - BETA_FIRST) * grad_sub
    second_new = BETA_SECOND * second + (1.0 - BETA_SECOND) * grad_sub * grad_sub
    first_hat = moment_new / (1.0 - BETA_FIRST**STEP)
    second_hat = second_new / (1.0 - BETA_SECOND**STEP)
    direction = first_hat / (jnp.sqrt(second_hat) + EPSILON)
    return (moment_new, second_new, direction)


def to_natural(v):
    return jnp.concatenate([v[:, zh * 128 + x * 32 : zh * 128 + x * 32 + 32] for x in range(4) for zh in range(2)], axis=1)


def to_halves(v):
    return jnp.concatenate([v[:, x * 64 + zh * 32 : x * 64 + zh * 32 + 32] for zh in range(2) for x in range(4)], axis=1)


def kernel(
    blk_hbm, x_hbm, go_hbm, mom_hbm, sec_hbm,
    upd, mnew, snew,
    x_v, go_v, mom, sec, got, raw, basis, own, out_p, pair_in, pre, suf, out_r, out_l, proj, btf, btb, cbuf, s1, rb, zsend, zrecv, total, direct, dirs,
    load_sem, z_send, z_recv, g_send, g_recv, c_send, c_recv, r_send, r_recv, l_send, l_recv, b_send, b_recv, d_send, d_recv, t_send, t_recv,
    p_send, p_recv, q_send, q_recv,
):
    d = lax.axis_index("dp")
    f = lax.axis_index("fsdp")
    core = lax.rem(d, 2)
    y = lax.rem(d // 2, 4)
    zh = lax.rem(d // 8, 2)
    xx = d // 16
    pos = xx * 4 + y
    pair = f // 2
    side = lax.rem(f, 2)
    other_side = (d, f + 1 - 2 * side)
    other_core = (d + 1 - 2 * core, f)
    other_zh = (d + 8 - 16 * zh, f)

    def at_pos(q):
        return (((q // 4) * 2 + zh) * 8 + lax.rem(q, 4) * 2 + core, f)

    barrier = pltpu.get_barrier_semaphore()
    pl.semaphore_signal(barrier, inc=1, device_id=other_zh, device_id_type=MESH)
    pl.semaphore_signal(barrier, inc=1, device_id=other_core, device_id_type=MESH)

    def greet_line(i, _):
        pl.semaphore_signal(barrier, inc=1, device_id=(d, lax.rem(f + i, LINE)), device_id_type=MESH)
        return 0

    lax.fori_loop(1, LINE, greet_line, 0)

    def greet(i, _):
        pl.semaphore_signal(barrier, inc=1, device_id=at_pos(lax.rem(pos + i, 16)), device_id_type=MESH)
        return 0

    lax.fori_loop(1, 16, greet, 0)

    load_x = pltpu.make_async_copy(x_hbm, x_v, load_sem.at[0])
    load_go = pltpu.make_async_copy(go_hbm, go_v, load_sem.at[1])
    load_mom = pltpu.make_async_copy(mom_hbm, mom, load_sem.at[2])
    load_sec = pltpu.make_async_copy(sec_hbm, sec, load_sem.at[3])
    load_blk = pltpu.make_async_copy(blk_hbm, raw.at[zh, core, pos], load_sem.at[4])
    load_blk.start()
    load_go.start()
    load_x.start()
    load_mom.start()
    load_sec.start()
    @pl.when(pair == 0)
    def _():
        pre[:] = jnp.zeros_like(pre)

    @pl.when(pair == PAIRS - 1)
    def _():
        suf[:] = jnp.zeros_like(suf)

    load_x.wait()
    load_mom.wait()
    load_sec.wait()
    load_go.wait()
    load_blk.wait()
    pl.semaphore_wait(barrier, 24)

    def send_block(which, i):
        q = lax.rem(pos + i, 16)
        return pltpu.make_async_remote_copy(
            raw.at[which, core, pos], raw.at[which, core, pos], g_send.at[which, i], g_recv.at[which, pos],
            device_id=at_pos(q), device_id_type=MESH)

    def wait_block(which, i):
        q = lax.rem(pos + 16 - i, 16)
        pltpu.make_async_remote_copy(
            raw.at[which, core, q], raw.at[which, core, q], g_send.at[which, i], g_recv.at[which, q],
            device_id=at_pos(q), device_id_type=MESH).wait_recv()

    def each_peer(action):
        def body(i, _):
            action(i)
            return 0
        lax.fori_loop(1, 16, body, 0)

    swap_zh = pltpu.make_async_remote_copy(
        raw.at[zh, core, pos], raw.at[zh, core, pos], z_send.at[0], z_recv.at[0], device_id=other_zh, device_id_type=MESH)
    swap_zh.start()
    each_peer(lambda i: send_block(zh, i).start())

    def swap_core(which):
        return pltpu.make_async_remote_copy(
            raw.at[which, core], raw.at[which, core], c_send.at[which], c_recv.at[which],
            device_id=other_core, device_id_type=MESH)

    def turn(i, _):
        cols = pl.ds(pl.multiple_of(i * 128, 128), 128)
        got[cols, :] = go_v[:, cols].T
        return 0

    lax.fori_loop(0, UNITS // 128, turn, 0)

    each_peer(lambda i: wait_block(zh, i))
    swap_core(zh).start()
    swap_zh.wait_recv()
    each_peer(lambda i: send_block(1 - zh, i).start())

    row = lax.broadcasted_iota(jnp.int32, (256, 256), 0)
    col = lax.broadcasted_iota(jnp.int32, (256, 256), 1)
    source = ((row // 4) % 2) * 128 + ((row // 8) % 4) * 32 + (row // 32) * 4 + row % 4
    perm = jnp.where(col == source, 1.0, 0.0).astype(BF16)

    def unfold(which):
        for x in range(4):
            blocks = jnp.concatenate(
                [raw[which, 0, 4 * x : 4 * x + 4].reshape(128, 128), raw[which, 1, 4 * x : 4 * x + 4].reshape(128, 128)], axis=0)
            placed = jnp.dot(perm, blocks, preferred_element_type=F32).astype(BF16)
            for b in range(8):
                basis[which, 32 * x : 32 * x + 32, 128 * b : 128 * b + 128] = placed[32 * b : 32 * b + 32]

    def project(which):
        own[which] = lax.dot_general(
            x_v[...], basis[which], (((1,), (1,)), ((), ())), preferred_element_type=F32)

    swap_core(zh).wait()
    unfold(zh)
    project(zh)

    def mine_at(p):
        return pl.ds(pl.multiple_of(side * SHARE + p * PIECE, PIECE), PIECE)

    def give(which, p):
        rows = pl.ds(pl.multiple_of(p * PIECE, PIECE), PIECE)
        return pltpu.make_async_remote_copy(
            out_p.at[which, rows], pair_in.at[which, rows], p_send.at[which, p], p_recv.at[which, p],
            device_id=other_side, device_id_type=MESH)

    def right(which, p):
        rows = pl.ds(pl.multiple_of(p * PIECE, PIECE), PIECE)
        return pltpu.make_async_remote_copy(
            out_r.at[which, rows], pre.at[which, rows], r_send.at[which, p], r_recv.at[which, p],
            device_id=(d, lax.rem(f + 2, LINE)), device_id_type=MESH)

    def left(which, p):
        rows = pl.ds(pl.multiple_of(p * PIECE, PIECE), PIECE)
        return pltpu.make_async_remote_copy(
            out_l.at[which, rows], suf.at[which, rows], l_send.at[which, p], l_recv.at[which, p],
            device_id=(d, lax.rem(f + LINE - 2, LINE)), device_id_type=MESH)

    def share(which, p):
        rows = mine_at(p)
        return pltpu.make_async_remote_copy(
            proj.at[which, rows], proj.at[which, rows], q_send.at[which, p], q_recv.at[which, p],
            device_id=other_side, device_id_type=MESH)

    def shared(which, p):
        rows = pl.ds(pl.multiple_of((1 - side) * SHARE + p * PIECE, PIECE), PIECE)
        return pltpu.make_async_remote_copy(
            proj.at[which, rows], proj.at[which, rows], q_send.at[which, p], q_recv.at[which, p],
            device_id=other_side, device_id_type=MESH)

    far = jnp.maximum(pair, PAIRS - 1 - pair)

    def chain(which, t):
        @pl.when((t >= 0) & (t < PIECES))
        def _():
            rows = pl.ds(pl.multiple_of(t * PIECE, PIECE), PIECE)
            theirs = pl.ds(pl.multiple_of((1 - side) * SHARE + t * PIECE, PIECE), PIECE)
            out_p[which, rows] = own[which, theirs].astype(BF16)
            give(which, t).start()

        m = t - MERGED

        @pl.when((m >= 0) & (m < PIECES))
        def _():
            give(which, m).wait_recv()
            rows = pl.ds(pl.multiple_of(m * PIECE, PIECE), PIECE)
            own[which, mine_at(m)] += pair_in[which, rows].astype(F32)

        p = m - pair * SKEW

        @pl.when((p >= 0) & (p < PIECES))
        def _():
            @pl.when(pair > 0)
            def _():
                right(which, p).wait_recv()

            @pl.when(pair < PAIRS - 1)
            def _():
                rows = pl.ds(pl.multiple_of(p * PIECE, PIECE), PIECE)
                out_r[which, rows] = (own[which, mine_at(p)] + pre[which, rows].astype(F32)).astype(BF16)
                right(which, p).start()

        q = m - (PAIRS - 1 - pair) * SKEW

        @pl.when((q >= 0) & (q < PIECES))
        def _():
            @pl.when(pair < PAIRS - 1)
            def _():
                left(which, q).wait_recv()

            @pl.when(pair > 0)
            def _():
                rows = pl.ds(pl.multiple_of(q * PIECE, PIECE), PIECE)
                out_l[which, rows] = (own[which, mine_at(q)] + suf[which, rows].astype(F32)).astype(BF16)
                left(which, q).start()

        e = m - far * SKEW

        @pl.when((e >= 0) & (e < PIECES))
        def _():
            rows = pl.ds(pl.multiple_of(e * PIECE, PIECE), PIECE)
            proj[which, mine_at(e)] = (
                own[which, mine_at(e)] + (pre[which, rows].astype(F32) + suf[which, rows].astype(F32))).astype(BF16)
            share(which, e).start()

    btf[224:, :] = jnp.zeros((8, 128), F32)

    def swap_terms(which, z, x):
        rows = pl.ds(x * 4, 4)
        return pltpu.make_async_remote_copy(
            btb.at[which, 1 - core, z, rows], cbuf.at[which, z, rows], t_send.at[which, z, x], t_recv.at[which, z, x],
            device_id=other_core, device_id_type=MESH)

    def turn_of(i):
        return (lax.rem(1 - zh + i // 4, 2), lax.rem(xx + 1 + i, 4))

    def all_shared(which):
        def arrived(p, _):
            shared(which, p).wait_recv()
            return 0

        lax.fori_loop(0, PIECES, arrived, 0)

    def terms_of(which):
        def terms(i, _):
            z, x = turn_of(i)
            first = pl.multiple_of(x * 448 + z * 224, 32)
            btf[0:224, :] = jnp.dot(got[pl.ds(first, 224), :], proj[which], preferred_element_type=F32)
            for k in range(4):
                two = btf[56 * k : 56 * k + 64, :]
                btb[which, 0, z, x * 4 + k] = two[:PAD].astype(BF16)
                btb[which, 1, z, x * 4 + k] = pltpu.roll(two, 64 - OWNED, 0)[:PAD].astype(BF16)
            swap_terms(which, z, x).start()
            return 0

        return terms

    def make_terms(which):
        all_shared(which)
        lax.fori_loop(0, 8, terms_of(which), 0)

    def send_terms(which, z, q):
        return pltpu.make_async_remote_copy(
            s1.at[which, z, q], rb.at[which, z, pos], b_send.at[which, z, q], b_recv.at[which, z, pos],
            device_id=at_pos(q), device_id_type=MESH)

    def send_both(which, q):
        return pltpu.make_async_remote_copy(
            s1.at[which, pl.ds(0, 2), q], rb.at[which, pl.ds(0, 2), pos], b_send.at[which, 0, q], b_recv.at[which, 0, pos],
            device_id=at_pos(q), device_id_type=MESH)

    def add_cores_first(which):
        def body(i, _):
            x = lax.rem(xx + 1 + i, 4)
            for z in range(2):
                swap_terms(which, z, x).wait()
            for k in range(4):
                q = x * 4 + lax.rem(y + 1 + k, 4)
                for z in range(2):
                    s1[which, z, q] = (btb[which, core, z, q].astype(F32) + cbuf[which, z, q].astype(F32)).astype(BF16)

                @pl.when(q != pos)
                def _():
                    send_both(which, q).start()

            return 0

        lax.fori_loop(0, 4, body, 0)

    def make_and_add(which):
        terms = terms_of(which)

        def body(step, _):
            @pl.when(step < 8)
            def _():
                terms(step, 0)

            @pl.when(step >= BEHIND)
            def _():
                add(step - BEHIND)

            return 0

        def add(i):
            z, x = turn_of(i)
            swap_terms(which, z, x).wait()
            for k in range(4):
                q = x * 4 + lax.rem(y + 1 + k, 4)
                s1[which, z, q] = (btb[which, core, z, q].astype(F32) + cbuf[which, z, q].astype(F32)).astype(BF16)

                @pl.when(q != pos)
                def _():
                    send_terms(which, z, q).start()

        all_shared(which)
        lax.fori_loop(0, 8 + BEHIND, body, 0)

    first_done = MERGED + far * SKEW + PIECES + (far - 2) * MERGED + (3 - far) * (LATER + 1)

    def step(t, _):
        chain(zh, t)
        chain(1 - zh, t - LATER)

        @pl.when(t == GATHERED)
        def _():
            each_peer(lambda i: wait_block(1 - zh, i))
            swap_core(1 - zh).start()

        @pl.when(t == PROJECTED)
        def _():
            swap_core(1 - zh).wait()
            unfold(1 - zh)
            project(1 - zh)

        @pl.when(t == first_done)
        def _():
            make_terms(zh)

        @pl.when(t == first_done + ADDED)
        def _():
            add_cores_first(zh)

        return 0

    lax.fori_loop(0, LATER + MERGED + (PAIRS - 1) * SKEW + PIECES + ADDED, step, 0)
    make_and_add(1 - zh)

    def swap_sum(which):
        return pltpu.make_async_remote_copy(
            zsend.at[which], zrecv.at[which], z_send.at[1 + which], z_recv.at[1 + which],
            device_id=other_zh, device_id_type=MESH)

    def add_chips(which, z):
        def body(i, acc):
            q = lax.rem(pos + 16 - i, 16)
            pltpu.make_async_remote_copy(
                s1.at[which, z, q], rb.at[which, z, q], b_send.at[which, z, q], b_recv.at[which, z, q],
                device_id=at_pos(q), device_id_type=MESH).wait_recv()
            return acc + rb[which, z, q].astype(F32)

        return lax.fori_loop(1, 16, body, s1[which, z, pos].astype(F32))

    def add_chips_first(which):
        def body(i, acc):
            q = lax.rem(pos + 16 - i, 16)
            pltpu.make_async_remote_copy(
                s1.at[which, pl.ds(0, 2), q], rb.at[which, pl.ds(0, 2), q], b_send.at[which, 0, q], b_recv.at[which, 0, q],
                device_id=at_pos(q), device_id_type=MESH).wait_recv()
            return (acc[0] + rb[which, zh, q].astype(F32), acc[1] + rb[which, 1 - zh, q].astype(F32))

        return lax.fori_loop(1, 16, body, (s1[which, zh, pos].astype(F32), s1[which, 1 - zh, pos].astype(F32)))

    mine, theirs = add_chips_first(zh)
    total[zh] = mine
    zsend[zh] = theirs.astype(BF16)
    swap_sum(zh).start()
    zsend[1 - zh] = add_chips(1 - zh, 1 - zh).astype(BF16)
    swap_sum(1 - zh).start()
    total[1 - zh] = add_chips(1 - zh, zh)
    swap_sum(zh).wait()
    swap_sum(1 - zh).wait()
    grad_sub = to_natural(jnp.concatenate([total[h] + zrecv[h].astype(F32) for h in range(2)], axis=1))[:OWNED]

    moment_new, second_new, direction = adam_direction(grad_sub, mom[...], sec[...])
    mnew[...] = moment_new
    snew[...] = second_new
    direct[OWNED - 4 :, :] = jnp.zeros((PAD - OWNED + 4, RANK), F32)
    direct[:OWNED, :] = to_halves(direction)
    dirs[f] = direct[...].astype(BF16)

    def send_dir(i):
        return pltpu.make_async_remote_copy(
            dirs.at[f], dirs.at[f], d_send.at[i], d_recv.at[f],
            device_id=(d, lax.rem(f + i, LINE)), device_id_type=MESH)

    def each_line(action):
        def body(i, _):
            action(i)
            return 0
        lax.fori_loop(1, LINE, body, 0)

    each_line(lambda i: send_dir(i).start())

    def wait_dir(i):
        q = lax.rem(f + LINE - i, LINE)
        pltpu.make_async_remote_copy(
            dirs.at[q], dirs.at[q], d_send.at[i], d_recv.at[q], device_id=(d, q), device_id_type=MESH).wait_recv()

    each_line(wait_dir)
    both = basis[...].reshape(RANK, FEATURES)
    row = lax.broadcasted_iota(jnp.int32, (OWNED * LINE, LINE * PAD), 0)
    col = lax.broadcasted_iota(jnp.int32, (OWNED * LINE, LINE * PAD), 1)
    order = jnp.where(col == (row % LINE) * PAD + row // LINE, 1.0, 0.0).astype(BF16)
    ordered = jnp.dot(order, dirs[...].reshape(LINE * PAD, RANK), preferred_element_type=F32).astype(BF16)
    upd[...] = jnp.dot(ordered, both, preferred_element_type=F32).astype(BF16)

    swap_zh.wait_send()
    each_line(lambda i: send_dir(i).wait_send())
    each_peer(lambda i: send_both(zh, lax.rem(pos + i, 16)).wait_send())
    for z in range(2):
        each_peer(lambda i: send_terms(1 - zh, z, lax.rem(pos + i, 16)).wait_send())
    for which in range(2):
        each_peer(lambda i: send_block(which, i).wait_send())

        def sent(p, _):
            give(which, p).wait_send()
            share(which, p).wait_send()

            @pl.when(pair < PAIRS - 1)
            def _():
                right(which, p).wait_send()

            @pl.when(pair > 0)
            def _():
                left(which, p).wait_send()

            return 0

        lax.fori_loop(0, PIECES, sent, 0)


def local(inputs, grad_out, projector, moment, second):
    blk = projector.T.reshape(4, 8, 128).transpose(1, 0, 2).reshape(32, 128)
    vmem = pl.BlockSpec(memory_space=pltpu.VMEM)
    anywhere = pl.BlockSpec(memory_space=pl.ANY)
    dma = pltpu.SemaphoreType.DMA
    update, moment_new, second_new = pl.pallas_call(
        kernel,
        out_shape=(
            jax.ShapeDtypeStruct((OWNED * LINE, FEATURES), BF16),
            jax.ShapeDtypeStruct((OWNED, RANK), F32),
            jax.ShapeDtypeStruct((OWNED, RANK), F32),
        ),
        in_specs=[anywhere, anywhere, anywhere, anywhere, anywhere],
        out_specs=(vmem, vmem, vmem),
        scratch_shapes=[
            pltpu.VMEM((TOKENS, FEATURES), BF16),
            pltpu.VMEM((TOKENS, UNITS), BF16),
            pltpu.VMEM((OWNED, RANK), F32),
            pltpu.VMEM((OWNED, RANK), F32),
            pltpu.VMEM((UNITS, TOKENS), BF16),
            pltpu.VMEM((2, 2, 16, 32, 128), BF16),
            pltpu.VMEM((2, 128, FEATURES), BF16),
            pltpu.VMEM((2, TOKENS, 128), F32),
            pltpu.VMEM((2, SHARE, 128), BF16),
            pltpu.VMEM((2, SHARE, 128), BF16),
            pltpu.VMEM((2, SHARE, 128), BF16),
            pltpu.VMEM((2, SHARE, 128), BF16),
            pltpu.VMEM((2, SHARE, 128), BF16),
            pltpu.VMEM((2, SHARE, 128), BF16),
            pltpu.VMEM((2, TOKENS, 128), BF16),
            pltpu.VMEM((232, 128), F32),
            pltpu.VMEM((2, 2, 2, 16, PAD, 128), BF16),
            pltpu.VMEM((2, 2, 16, PAD, 128), BF16),
            pltpu.VMEM((2, 2, 16, PAD, 128), BF16),
            pltpu.VMEM((2, 2, 16, PAD, 128), BF16),
            pltpu.VMEM((2, PAD, 128), BF16),
            pltpu.VMEM((2, PAD, 128), BF16),
            pltpu.VMEM((2, PAD, 128), F32),
            pltpu.VMEM((PAD, RANK), F32),
            pltpu.VMEM((LINE, PAD, RANK), BF16),
            dma((5,)),
            dma((3,)), dma((3,)),
            dma((2, 16)), dma((2, 16)),
            dma((2,)), dma((2,)),
            dma((2, PIECES)), dma((2, PIECES)), dma((2, PIECES)), dma((2, PIECES)),
            dma((2, 2, 16)), dma((2, 2, 16)),
            dma((LINE,)), dma((LINE,)),
            dma((2, 2, 4)), dma((2, 2, 4)),
            dma((2, PIECES)), dma((2, PIECES)), dma((2, PIECES)), dma((2, PIECES)),
        ],
        compiler_params=pltpu.CompilerParams(
            collective_id=0, has_side_effects=True, vmem_limit_bytes=48 * 1024 * 1024),
    )(*[pltpu.with_memory_space_constraint(v, pltpu.HBM) for v in (blk, inputs, grad_out, moment, second)])
    return (update.reshape(OWNED, LINE, FEATURES).transpose(1, 0, 2), moment_new, second_new)


def solution(mesh):
    return jax.shard_map(
        local,
        mesh=mesh,
        in_specs=(
            P("dp", "fsdp"),
            P("dp", "fsdp"),
            P("fsdp", "dp"),
            P(("fsdp", "dp"), None),
            P(("fsdp", "dp"), None),
        ),
        out_specs=(P(None, "dp", "fsdp"), P(("fsdp", "dp"), None), P(("fsdp", "dp"), None)),
        check_vma=False,
    )
```

```python
import functools

import jax
import jax.numpy as jnp
from jax import lax
from jax.experimental import pallas as pl
from jax.experimental.pallas import tpu as pltpu
from jax.sharding import PartitionSpec as P

MESH = pl.DeviceIdType.MESH
F32 = jnp.float32
BF16 = jnp.bfloat16

STEP = 10
BETA_FIRST = 0.9
BETA_SECOND = 0.999
EPSILON = 1e-08

TOKENS = 768
FEATURES = 1024
UNITS = 1792
RANK = 256
OWNED = 28
PAD = 32
LINE = 8
PAIRS = LINE // 2
SHARE = TOKENS // 2
PIECE = 128
PIECES = SHARE // PIECE
MERGED = 3
SKEW = 4
GATHERED = 4
PROJECTED = 5
LATER = 7
ADDED = 4
BEHIND = 3


def adam_direction(grad_sub, moment, second):
    moment_new = BETA_FIRST * moment + (1.0 - BETA_FIRST) * grad_sub
    second_new = BETA_SECOND * second + (1.0 - BETA_SECOND) * grad_sub * grad_sub
    first_hat = moment_new / (1.0 - BETA_FIRST**STEP)
    second_hat = second_new / (1.0 - BETA_SECOND**STEP)
    direction = first_hat / (jnp.sqrt(second_hat) + EPSILON)
    return (moment_new, second_new, direction)


def to_natural(v):
    return jnp.concatenate([v[:, zh * 128 + x * 32 : zh * 128 + x * 32 + 32] for x in range(4) for zh in range(2)], axis=1)


def to_halves(v):
    return jnp.concatenate([v[:, x * 64 + zh * 32 : x * 64 + zh * 32 + 32] for zh in range(2) for x in range(4)], axis=1)


def kernel(
    blk_hbm, x_hbm, go_hbm, mom_hbm, sec_hbm,
    upd, grad,
    x_v, go_v, mom, sec, got, raw, basis, own, out_p, pair_in, pre, suf, out_r, out_l, proj, early, btf, btb, cbuf, s1, rb, zsend, zrecv, total, direct, dirs,
    load_sem, z_send, z_recv, g_send, g_recv, c_send, c_recv, r_send, r_recv, l_send, l_recv, b_send, b_recv, d_send, d_recv, t_send, t_recv,
    p_send, p_recv, q_send, q_recv,
):
    d = lax.axis_index("dp")
    f = lax.axis_index("fsdp")
    core = lax.rem(d, 2)
    y = lax.rem(d // 2, 4)
    zh = lax.rem(d // 8, 2)
    xx = d // 16
    pos = xx * 4 + y
    pair = f // 2
    side = lax.rem(f, 2)
    other_side = (d, f + 1 - 2 * side)
    other_core = (d + 1 - 2 * core, f)
    other_zh = (d + 8 - 16 * zh, f)

    def at_pos(q):
        return (((q // 4) * 2 + zh) * 8 + lax.rem(q, 4) * 2 + core, f)

    barrier = pltpu.get_barrier_semaphore()
    pl.semaphore_signal(barrier, inc=1, device_id=other_zh, device_id_type=MESH)
    pl.semaphore_signal(barrier, inc=1, device_id=other_core, device_id_type=MESH)

    def greet_line(i, _):
        pl.semaphore_signal(barrier, inc=1, device_id=(d, lax.rem(f + i, LINE)), device_id_type=MESH)
        return 0

    lax.fori_loop(1, LINE, greet_line, 0)

    def greet(i, _):
        pl.semaphore_signal(barrier, inc=1, device_id=at_pos(lax.rem(pos + i, 16)), device_id_type=MESH)
        return 0

    lax.fori_loop(1, 16, greet, 0)

    load_x = pltpu.make_async_copy(x_hbm, x_v, load_sem.at[0])
    load_go = pltpu.make_async_copy(go_hbm, go_v, load_sem.at[1])
    load_mom = pltpu.make_async_copy(mom_hbm, mom, load_sem.at[2])
    load_sec = pltpu.make_async_copy(sec_hbm, sec, load_sem.at[3])
    load_blk = pltpu.make_async_copy(blk_hbm, raw.at[zh, core, pos], load_sem.at[4])
    load_blk.start()
    load_go.start()
    load_x.start()
    load_mom.start()
    load_sec.start()

    load_blk.wait()
    pl.semaphore_wait(barrier, 24)

    def send_block(which, i):
        q = lax.rem(pos + i, 16)
        return pltpu.make_async_remote_copy(
            raw.at[which, core, pos], raw.at[which, core, pos], g_send.at[which, i], g_recv.at[which, pos],
            device_id=at_pos(q), device_id_type=MESH)

    def wait_block(which, i):
        q = lax.rem(pos + 16 - i, 16)
        pltpu.make_async_remote_copy(
            raw.at[which, core, q], raw.at[which, core, q], g_send.at[which, i], g_recv.at[which, q],
            device_id=at_pos(q), device_id_type=MESH).wait_recv()

    def each_peer(action):
        def body(i, _):
            action(i)
            return 0
        lax.fori_loop(1, 16, body, 0)

    swap_zh = pltpu.make_async_remote_copy(
        raw.at[zh, core, pos], raw.at[zh, core, pos], z_send.at[0], z_recv.at[0], device_id=other_zh, device_id_type=MESH)
    swap_zh.start()
    each_peer(lambda i: send_block(zh, i).start())

    def swap_core(which):
        return pltpu.make_async_remote_copy(
            raw.at[which, core], raw.at[which, core], c_send.at[which], c_recv.at[which],
            device_id=other_core, device_id_type=MESH)

    def turn(i, _):
        cols = pl.ds(pl.multiple_of(i * 128, 128), 128)
        got[cols, :] = go_v[:, cols].T
        return 0

    load_go.wait()
    lax.fori_loop(0, UNITS // 128, turn, 0)

    @pl.when(pair == 0)
    def _():
        pre[:] = jnp.zeros_like(pre)

    @pl.when(pair == PAIRS - 1)
    def _():
        suf[:] = jnp.zeros_like(suf)

    each_peer(lambda i: wait_block(zh, i))
    swap_core(zh).start()
    swap_zh.wait_recv()
    each_peer(lambda i: send_block(1 - zh, i).start())

    row = lax.broadcasted_iota(jnp.int32, (256, 256), 0)
    col = lax.broadcasted_iota(jnp.int32, (256, 256), 1)
    source = ((row // 4) % 2) * 128 + ((row // 8) % 4) * 32 + (row // 32) * 4 + row % 4
    perm = jnp.where(col == source, 1.0, 0.0).astype(BF16)

    def unfold(which):
        for x in range(4):
            blocks = jnp.concatenate(
                [raw[which, 0, 4 * x : 4 * x + 4].reshape(128, 128), raw[which, 1, 4 * x : 4 * x + 4].reshape(128, 128)], axis=0)
            placed = jnp.dot(perm, blocks, preferred_element_type=F32).astype(BF16)
            for b in range(8):
                basis[which, 32 * x : 32 * x + 32, 128 * b : 128 * b + 128] = placed[32 * b : 32 * b + 32]

    def project(which):
        own[which] = lax.dot_general(
            x_v[...], basis[which], (((1,), (1,)), ((), ())), preferred_element_type=F32)

    load_x.wait()
    load_mom.wait()
    load_sec.wait()
    swap_core(zh).wait()
    unfold(zh)
    project(zh)

    def mine_at(p):
        return pl.ds(pl.multiple_of(side * SHARE + p * PIECE, PIECE), PIECE)

    def give(which, p):
        rows = pl.ds(pl.multiple_of(p * PIECE, PIECE), PIECE)
        return pltpu.make_async_remote_copy(
            out_p.at[which, rows], pair_in.at[which, rows], p_send.at[which, p], p_recv.at[which, p],
            device_id=other_side, device_id_type=MESH)

    def right(which, p):
        rows = pl.ds(pl.multiple_of(p * PIECE, PIECE), PIECE)
        return pltpu.make_async_remote_copy(
            out_r.at[which, rows], pre.at[which, rows], r_send.at[which, p], r_recv.at[which, p],
            device_id=(d, lax.rem(f + 2, LINE)), device_id_type=MESH)

    def left(which, p):
        rows = pl.ds(pl.multiple_of(p * PIECE, PIECE), PIECE)
        return pltpu.make_async_remote_copy(
            out_l.at[which, rows], suf.at[which, rows], l_send.at[which, p], l_recv.at[which, p],
            device_id=(d, lax.rem(f + LINE - 2, LINE)), device_id_type=MESH)

    def share(which, p):
        rows = mine_at(p)
        return pltpu.make_async_remote_copy(
            proj.at[which, rows], proj.at[which, rows], q_send.at[which, p], q_recv.at[which, p],
            device_id=other_side, device_id_type=MESH)

    def shared(which, p):
        rows = pl.ds(pl.multiple_of((1 - side) * SHARE + p * PIECE, PIECE), PIECE)
        return pltpu.make_async_remote_copy(
            proj.at[which, rows], proj.at[which, rows], q_send.at[which, p], q_recv.at[which, p],
            device_id=other_side, device_id_type=MESH)

    far = jnp.maximum(pair, PAIRS - 1 - pair)

    def chain(which, t):
        @pl.when((t >= 0) & (t < PIECES))
        def _():
            rows = pl.ds(pl.multiple_of(t * PIECE, PIECE), PIECE)
            theirs = pl.ds(pl.multiple_of((1 - side) * SHARE + t * PIECE, PIECE), PIECE)
            out_p[which, rows] = own[which, theirs].astype(BF16)
            give(which, t).start()

        m = t - MERGED

        @pl.when((m >= 0) & (m < PIECES))
        def _():
            give(which, m).wait_recv()
            rows = pl.ds(pl.multiple_of(m * PIECE, PIECE), PIECE)
            own[which, mine_at(m)] += pair_in[which, rows].astype(F32)

        p = m - pair * SKEW

        @pl.when((p >= 0) & (p < PIECES))
        def _():
            @pl.when(pair > 0)
            def _():
                right(which, p).wait_recv()

            @pl.when(pair < PAIRS - 1)
            def _():
                rows = pl.ds(pl.multiple_of(p * PIECE, PIECE), PIECE)
                out_r[which, rows] = (own[which, mine_at(p)] + pre[which, rows].astype(F32)).astype(BF16)
                right(which, p).start()

        q = m - (PAIRS - 1 - pair) * SKEW

        @pl.when((q >= 0) & (q < PIECES))
        def _():
            @pl.when(pair < PAIRS - 1)
            def _():
                left(which, q).wait_recv()

            @pl.when(pair > 0)
            def _():
                rows = pl.ds(pl.multiple_of(q * PIECE, PIECE), PIECE)
                out_l[which, rows] = (own[which, mine_at(q)] + suf[which, rows].astype(F32)).astype(BF16)
                left(which, q).start()

        e = m - far * SKEW

        @pl.when((e >= 0) & (e < PIECES))
        def _():
            rows = pl.ds(pl.multiple_of(e * PIECE, PIECE), PIECE)
            proj[which, mine_at(e)] = (
                own[which, mine_at(e)] + (pre[which, rows].astype(F32) + suf[which, rows].astype(F32))).astype(BF16)
            share(which, e).start()

    btf[224:, :] = jnp.zeros((8, 128), F32)

    def swap_terms(which, z, x):
        rows = pl.ds(x * 4, 4)
        return pltpu.make_async_remote_copy(
            btb.at[which, 1 - core, z, rows], cbuf.at[which, z, rows], t_send.at[which, z, x], t_recv.at[which, z, x],
            device_id=other_core, device_id_type=MESH)

    def turn_of(i):
        return (lax.rem(1 - zh + i // 4, 2), lax.rem(xx + 1 + i, 4))

    def all_shared(which):
        def arrived(p, _):
            shared(which, p).wait_recv()
            return 0

        lax.fori_loop(0, PIECES, arrived, 0)

    mine_half = pl.ds(pl.multiple_of(side * SHARE, 128), SHARE)
    their_half = pl.ds(pl.multiple_of((1 - side) * SHARE, 128), SHARE)

    def early_terms(which):
        def body(i, _):
            rows = pl.ds(pl.multiple_of(i * 448, 32), 448)
            early[rows, :] = jnp.dot(got[rows, mine_half], proj[which, mine_half], preferred_element_type=F32)
            return 0

        lax.fori_loop(0, 4, body, 0)

    def terms_of(which):
        def terms(i, _):
            z, x = turn_of(i)
            first = pl.multiple_of(x * 448 + z * 224, 32)
            rows = pl.ds(first, 224)
            btf[0:224, :] = early[rows, :] + jnp.dot(got[rows, their_half], proj[which, their_half], preferred_element_type=F32)
            for k in range(4):
                two = btf[56 * k : 56 * k + 64, :]
                btb[which, 0, z, x * 4 + k] = two[:PAD].astype(BF16)
                btb[which, 1, z, x * 4 + k] = pltpu.roll(two, 64 - OWNED, 0)[:PAD].astype(BF16)
            swap_terms(which, z, x).start()
            return 0

        return terms

    def make_terms(which):
        early_terms(which)
        all_shared(which)
        lax.fori_loop(0, 8, terms_of(which), 0)

    def send_terms(which, z, q):
        return pltpu.make_async_remote_copy(
            s1.at[which, z, q], rb.at[which, z, pos], b_send.at[which, z, q], b_recv.at[which, z, pos],
            device_id=at_pos(q), device_id_type=MESH)

    def send_both(which, q):
        return pltpu.make_async_remote_copy(
            s1.at[which, pl.ds(0, 2), q], rb.at[which, pl.ds(0, 2), pos], b_send.at[which, 0, q], b_recv.at[which, 0, pos],
            device_id=at_pos(q), device_id_type=MESH)

    def add_cores_first(which):
        def body(i, _):
            x = lax.rem(xx + 1 + i, 4)
            for z in range(2):
                swap_terms(which, z, x).wait()
            for k in range(4):
                q = x * 4 + lax.rem(y + 1 + k, 4)
                for z in range(2):
                    s1[which, z, q] = (btb[which, core, z, q].astype(F32) + cbuf[which, z, q].astype(F32)).astype(BF16)

                @pl.when(q != pos)
                def _():
                    send_both(which, q).start()

            return 0

        lax.fori_loop(0, 4, body, 0)

    def make_and_add(which):
        terms = terms_of(which)

        def body(step, _):
            @pl.when(step < 8)
            def _():
                terms(step, 0)

            @pl.when(step >= BEHIND)
            def _():
                add(step - BEHIND)

            return 0

        def add(i):
            z, x = turn_of(i)
            swap_terms(which, z, x).wait()
            for k in range(4):
                q = x * 4 + lax.rem(y + 1 + k, 4)
                s1[which, z, q] = (btb[which, core, z, q].astype(F32) + cbuf[which, z, q].astype(F32)).astype(BF16)

                @pl.when(q != pos)
                def _():
                    send_terms(which, z, q).start()

        early_terms(which)
        all_shared(which)
        lax.fori_loop(0, 8 + BEHIND, body, 0)

    first_done = MERGED + far * SKEW + PIECES + (far - 2) * MERGED + (3 - far) * (LATER + 1)

    def step(t, _):
        chain(zh, t)
        chain(1 - zh, t - LATER)

        @pl.when(t == GATHERED)
        def _():
            each_peer(lambda i: wait_block(1 - zh, i))
            swap_core(1 - zh).start()

        @pl.when(t == PROJECTED)
        def _():
            swap_core(1 - zh).wait()
            unfold(1 - zh)
            project(1 - zh)

        @pl.when(t == first_done)
        def _():
            make_terms(zh)

        @pl.when(t == first_done + ADDED)
        def _():
            add_cores_first(zh)

        return 0

    lax.fori_loop(0, LATER + MERGED + (PAIRS - 1) * SKEW + PIECES + ADDED, step, 0)
    make_and_add(1 - zh)

    def swap_sum(which):
        return pltpu.make_async_remote_copy(
            zsend.at[which], zrecv.at[which], z_send.at[1 + which], z_recv.at[1 + which],
            device_id=other_zh, device_id_type=MESH)

    def add_chips(which, z):
        def body(i, acc):
            q = lax.rem(pos + 16 - i, 16)
            pltpu.make_async_remote_copy(
                s1.at[which, z, q], rb.at[which, z, q], b_send.at[which, z, q], b_recv.at[which, z, q],
                device_id=at_pos(q), device_id_type=MESH).wait_recv()
            return acc + rb[which, z, q].astype(F32)

        return lax.fori_loop(1, 16, body, s1[which, z, pos].astype(F32))

    def add_chips_first(which):
        def body(i, acc):
            q = lax.rem(pos + 16 - i, 16)
            pltpu.make_async_remote_copy(
                s1.at[which, pl.ds(0, 2), q], rb.at[which, pl.ds(0, 2), q], b_send.at[which, 0, q], b_recv.at[which, 0, q],
                device_id=at_pos(q), device_id_type=MESH).wait_recv()
            return (acc[0] + rb[which, zh, q].astype(F32), acc[1] + rb[which, 1 - zh, q].astype(F32))

        return lax.fori_loop(1, 16, body, (s1[which, zh, pos].astype(F32), s1[which, 1 - zh, pos].astype(F32)))

    mine, theirs = add_chips_first(zh)
    total[zh] = mine
    zsend[zh] = theirs.astype(BF16)
    swap_sum(zh).start()
    zsend[1 - zh] = add_chips(1 - zh, 1 - zh).astype(BF16)
    swap_sum(1 - zh).start()
    total[1 - zh] = add_chips(1 - zh, zh)
    swap_sum(zh).wait()
    swap_sum(1 - zh).wait()
    grad_sub = to_natural(jnp.concatenate([total[h] + zrecv[h].astype(F32) for h in range(2)], axis=1))[:OWNED]

    _, _, direction = adam_direction(grad_sub, mom[...], sec[...])
    grad[...] = grad_sub
    direct[OWNED - 4 :, :] = jnp.zeros((PAD - OWNED + 4, RANK), F32)
    direct[:OWNED, :] = to_halves(direction)
    dirs[f] = direct[...].astype(BF16)

    def send_dir(i):
        return pltpu.make_async_remote_copy(
            dirs.at[f], dirs.at[f], d_send.at[i], d_recv.at[f],
            device_id=(d, lax.rem(f + i, LINE)), device_id_type=MESH)

    def each_line(action):
        def body(i, _):
            action(i)
            return 0
        lax.fori_loop(1, LINE, body, 0)

    each_line(lambda i: send_dir(i).start())

    def wait_dir(i):
        q = lax.rem(f + LINE - i, LINE)
        pltpu.make_async_remote_copy(
            dirs.at[q], dirs.at[q], d_send.at[i], d_recv.at[q], device_id=(d, q), device_id_type=MESH).wait_recv()

    each_line(wait_dir)
    both = basis[...].reshape(RANK, FEATURES)
    row = lax.broadcasted_iota(jnp.int32, (OWNED * LINE, LINE * PAD), 0)
    col = lax.broadcasted_iota(jnp.int32, (OWNED * LINE, LINE * PAD), 1)
    order = jnp.where(col == (row % LINE) * PAD + row // LINE, 1.0, 0.0).astype(BF16)
    ordered = jnp.dot(order, dirs[...].reshape(LINE * PAD, RANK), preferred_element_type=F32).astype(BF16)
    upd[...] = jnp.dot(ordered, both, preferred_element_type=F32).astype(BF16)

    swap_zh.wait_send()
    each_line(lambda i: send_dir(i).wait_send())
    each_peer(lambda i: send_both(zh, lax.rem(pos + i, 16)).wait_send())
    for z in range(2):
        each_peer(lambda i: send_terms(1 - zh, z, lax.rem(pos + i, 16)).wait_send())
    for which in range(2):
        each_peer(lambda i: send_block(which, i).wait_send())

        def sent(p, _):
            give(which, p).wait_send()
            share(which, p).wait_send()

            @pl.when(pair < PAIRS - 1)
            def _():
                right(which, p).wait_send()

            @pl.when(pair > 0)
            def _():
                left(which, p).wait_send()

            return 0

        lax.fori_loop(0, PIECES, sent, 0)


def local(inputs, grad_out, projector, moment, second):
    blk = projector.T.reshape(4, 8, 128).transpose(1, 0, 2).reshape(32, 128)
    vmem = pl.BlockSpec(memory_space=pltpu.VMEM)
    anywhere = pl.BlockSpec(memory_space=pl.ANY)
    dma = pltpu.SemaphoreType.DMA
    update, grad_sub = pl.pallas_call(
        kernel,
        out_shape=(
            jax.ShapeDtypeStruct((OWNED * LINE, FEATURES), BF16),
            jax.ShapeDtypeStruct((OWNED, RANK), F32),
        ),
        in_specs=[anywhere, anywhere, anywhere, anywhere, anywhere],
        out_specs=(vmem, vmem),
        scratch_shapes=[
            pltpu.VMEM((TOKENS, FEATURES), BF16),
            pltpu.VMEM((TOKENS, UNITS), BF16),
            pltpu.VMEM((OWNED, RANK), F32),
            pltpu.VMEM((OWNED, RANK), F32),
            pltpu.VMEM((UNITS, TOKENS), BF16),
            pltpu.VMEM((2, 2, 16, 32, 128), BF16),
            pltpu.VMEM((2, 128, FEATURES), BF16),
            pltpu.VMEM((2, TOKENS, 128), F32),
            pltpu.VMEM((2, SHARE, 128), BF16),
            pltpu.VMEM((2, SHARE, 128), BF16),
            pltpu.VMEM((2, SHARE, 128), BF16),
            pltpu.VMEM((2, SHARE, 128), BF16),
            pltpu.VMEM((2, SHARE, 128), BF16),
            pltpu.VMEM((2, SHARE, 128), BF16),
            pltpu.VMEM((2, TOKENS, 128), BF16),
            pltpu.VMEM((UNITS, 128), F32),
            pltpu.VMEM((232, 128), F32),
            pltpu.VMEM((2, 2, 2, 16, PAD, 128), BF16),
            pltpu.VMEM((2, 2, 16, PAD, 128), BF16),
            pltpu.VMEM((2, 2, 16, PAD, 128), BF16),
            pltpu.VMEM((2, 2, 16, PAD, 128), BF16),
            pltpu.VMEM((2, PAD, 128), BF16),
            pltpu.VMEM((2, PAD, 128), BF16),
            pltpu.VMEM((2, PAD, 128), F32),
            pltpu.VMEM((PAD, RANK), F32),
            pltpu.VMEM((LINE, PAD, RANK), BF16),
            dma((5,)),
            dma((3,)), dma((3,)),
            dma((2, 16)), dma((2, 16)),
            dma((2,)), dma((2,)),
            dma((2, PIECES)), dma((2, PIECES)), dma((2, PIECES)), dma((2, PIECES)),
            dma((2, 2, 16)), dma((2, 2, 16)),
            dma((LINE,)), dma((LINE,)),
            dma((2, 2, 4)), dma((2, 2, 4)),
            dma((2, PIECES)), dma((2, PIECES)), dma((2, PIECES)), dma((2, PIECES)),
        ],
        compiler_params=pltpu.CompilerParams(
            collective_id=0, has_side_effects=True, vmem_limit_bytes=48 * 1024 * 1024),
    )(*[pltpu.with_memory_space_constraint(v, pltpu.HBM) for v in (blk, inputs, grad_out, moment, second)])
    moment_new, second_new, _ = adam_direction(grad_sub, moment, second)
    return (update.reshape(OWNED, LINE, FEATURES).transpose(1, 0, 2), moment_new, second_new)


def solution(mesh):
    return jax.shard_map(
        local,
        mesh=mesh,
        in_specs=(
            P("dp", "fsdp"),
            P("dp", "fsdp"),
            P("fsdp", "dp"),
            P(("fsdp", "dp"), None),
            P(("fsdp", "dp"), None),
        ),
        out_specs=(P(None, "dp", "fsdp"), P(("fsdp", "dp"), None), P(("fsdp", "dp"), None)),
        check_vma=False,
    )
```

```python
import functools

import jax
import jax.numpy as jnp
from jax import lax
from jax.experimental import pallas as pl
from jax.experimental.pallas import tpu as pltpu
from jax.sharding import PartitionSpec as P

MESH = pl.DeviceIdType.MESH
F32 = jnp.float32
BF16 = jnp.bfloat16

STEP = 10
BETA_FIRST = 0.9
BETA_SECOND = 0.999
EPSILON = 1e-08

TOKENS = 768
FEATURES = 1024
UNITS = 1792
RANK = 256
OWNED = 28
PAD = 32
LINE = 8
PAIRS = LINE // 2
SHARE = TOKENS // 2
PIECE = 128
PIECES = SHARE // PIECE
MERGED = 3
SKEW = 4
GATHERED = 4
PROJECTED = 5
LATER = 7
ADDED = 4
BEHIND = 3


def adam_direction(grad_sub, moment, second):
    moment_new = BETA_FIRST * moment + (1.0 - BETA_FIRST) * grad_sub
    second_new = BETA_SECOND * second + (1.0 - BETA_SECOND) * grad_sub * grad_sub
    first_hat = moment_new / (1.0 - BETA_FIRST**STEP)
    second_hat = second_new / (1.0 - BETA_SECOND**STEP)
    direction = first_hat / (jnp.sqrt(second_hat) + EPSILON)
    return (moment_new, second_new, direction)


def to_natural(v):
    return jnp.concatenate([v[:, zh * 128 + x * 32 : zh * 128 + x * 32 + 32] for x in range(4) for zh in range(2)], axis=1)


def to_halves(v):
    return jnp.concatenate([v[:, x * 64 + zh * 32 : x * 64 + zh * 32 + 32] for zh in range(2) for x in range(4)], axis=1)


def kernel(
    blk_hbm, x_hbm, go_hbm, mom_hbm, sec_hbm,
    upd, grad,
    x_v, go_v, mom, sec, got, raw, basis, own, out_p, pair_in, pre, suf, out_r, out_l, proj, early, btf, btb, cbuf, s1, rb, zsend, zrecv, total, direct, dirs,
    load_sem, z_send, z_recv, g_send, g_recv, c_send, c_recv, r_send, r_recv, l_send, l_recv, b_send, b_recv, d_send, d_recv, t_send, t_recv,
    p_send, p_recv, q_send, q_recv,
):
    d = lax.axis_index("dp")
    f = lax.axis_index("fsdp")
    core = lax.rem(d, 2)
    y = lax.rem(d // 2, 4)
    zh = lax.rem(d // 8, 2)
    xx = d // 16
    pos = xx * 4 + y
    pair = f // 2
    side = lax.rem(f, 2)
    other_side = (d, f + 1 - 2 * side)
    other_core = (d + 1 - 2 * core, f)
    other_zh = (d + 8 - 16 * zh, f)

    def at_pos(q):
        return (((q // 4) * 2 + zh) * 8 + lax.rem(q, 4) * 2 + core, f)

    barrier = pltpu.get_barrier_semaphore()
    pl.semaphore_signal(barrier, inc=1, device_id=other_zh, device_id_type=MESH)
    pl.semaphore_signal(barrier, inc=1, device_id=other_core, device_id_type=MESH)

    def greet_line(i, _):
        pl.semaphore_signal(barrier, inc=1, device_id=(d, lax.rem(f + i, LINE)), device_id_type=MESH)
        return 0

    lax.fori_loop(1, LINE, greet_line, 0)

    def greet(i, _):
        pl.semaphore_signal(barrier, inc=1, device_id=at_pos(lax.rem(pos + i, 16)), device_id_type=MESH)
        return 0

    lax.fori_loop(1, 16, greet, 0)

    load_x = pltpu.make_async_copy(x_hbm, x_v, load_sem.at[0])
    load_go = pltpu.make_async_copy(go_hbm, go_v, load_sem.at[1])
    load_mom = pltpu.make_async_copy(mom_hbm, mom, load_sem.at[2])
    load_sec = pltpu.make_async_copy(sec_hbm, sec, load_sem.at[3])
    load_blk = pltpu.make_async_copy(blk_hbm, raw.at[zh, core, pos], load_sem.at[4])
    load_blk.start()
    load_go.start()
    load_x.start()
    load_mom.start()
    load_sec.start()

    load_blk.wait()
    pl.semaphore_wait(barrier, 24)

    def send_block(which, i):
        q = lax.rem(pos + i, 16)
        return pltpu.make_async_remote_copy(
            raw.at[which, core, pos], raw.at[which, core, pos], g_send.at[which, i], g_recv.at[which, pos],
            device_id=at_pos(q), device_id_type=MESH)

    def wait_block(which, i):
        q = lax.rem(pos + 16 - i, 16)
        pltpu.make_async_remote_copy(
            raw.at[which, core, q], raw.at[which, core, q], g_send.at[which, i], g_recv.at[which, q],
            device_id=at_pos(q), device_id_type=MESH).wait_recv()

    def each_peer(action):
        def body(i, _):
            action(i)
            return 0
        lax.fori_loop(1, 16, body, 0)

    swap_zh = pltpu.make_async_remote_copy(
        raw.at[zh, core, pos], raw.at[zh, core, pos], z_send.at[0], z_recv.at[0], device_id=other_zh, device_id_type=MESH)
    swap_zh.start()
    each_peer(lambda i: send_block(zh, i).start())

    def swap_core(which):
        return pltpu.make_async_remote_copy(
            raw.at[which, core], raw.at[which, core], c_send.at[which], c_recv.at[which],
            device_id=other_core, device_id_type=MESH)

    def turn(i, _):
        cols = pl.ds(pl.multiple_of(i * 128, 128), 128)
        got[cols, :] = go_v[:, cols].T
        return 0

    load_go.wait()
    lax.fori_loop(0, UNITS // 128, turn, 0)

    @pl.when(pair == 0)
    def _():
        pre[:] = jnp.zeros_like(pre)

    @pl.when(pair == PAIRS - 1)
    def _():
        suf[:] = jnp.zeros_like(suf)

    each_peer(lambda i: wait_block(zh, i))
    swap_core(zh).start()
    swap_zh.wait_recv()
    each_peer(lambda i: send_block(1 - zh, i).start())

    row = lax.broadcasted_iota(jnp.int32, (256, 256), 0)
    col = lax.broadcasted_iota(jnp.int32, (256, 256), 1)
    source = ((row // 4) % 2) * 128 + ((row // 8) % 4) * 32 + (row // 32) * 4 + row % 4
    perm = jnp.where(col == source, 1.0, 0.0).astype(BF16)

    def unfold(which):
        for x in range(4):
            blocks = jnp.concatenate(
                [raw[which, 0, 4 * x : 4 * x + 4].reshape(128, 128), raw[which, 1, 4 * x : 4 * x + 4].reshape(128, 128)], axis=0)
            placed = jnp.dot(perm, blocks, preferred_element_type=F32).astype(BF16)
            for b in range(8):
                basis[which, 32 * x : 32 * x + 32, 128 * b : 128 * b + 128] = placed[32 * b : 32 * b + 32]

    def project(which):
        own[which] = lax.dot_general(
            x_v[...], basis[which], (((1,), (1,)), ((), ())), preferred_element_type=F32)

    load_x.wait()
    load_mom.wait()
    load_sec.wait()
    swap_core(zh).wait()
    unfold(zh)
    project(zh)

    def mine_at(p):
        return pl.ds(pl.multiple_of(side * SHARE + p * PIECE, PIECE), PIECE)

    def give(which, p):
        rows = pl.ds(pl.multiple_of(p * PIECE, PIECE), PIECE)
        return pltpu.make_async_remote_copy(
            out_p.at[which, rows], pair_in.at[which, rows], p_send.at[which, p], p_recv.at[which, p],
            device_id=other_side, device_id_type=MESH)

    def right(which, p):
        rows = pl.ds(pl.multiple_of(p * PIECE, PIECE), PIECE)
        return pltpu.make_async_remote_copy(
            out_r.at[which, rows], pre.at[which, rows], r_send.at[which, p], r_recv.at[which, p],
            device_id=(d, lax.rem(f + 2, LINE)), device_id_type=MESH)

    def left(which, p):
        rows = pl.ds(pl.multiple_of(p * PIECE, PIECE), PIECE)
        return pltpu.make_async_remote_copy(
            out_l.at[which, rows], suf.at[which, rows], l_send.at[which, p], l_recv.at[which, p],
            device_id=(d, lax.rem(f + LINE - 2, LINE)), device_id_type=MESH)

    def share(which, p):
        rows = mine_at(p)
        return pltpu.make_async_remote_copy(
            proj.at[which, rows], proj.at[which, rows], q_send.at[which, p], q_recv.at[which, p],
            device_id=other_side, device_id_type=MESH)

    def shared(which, p):
        rows = pl.ds(pl.multiple_of((1 - side) * SHARE + p * PIECE, PIECE), PIECE)
        return pltpu.make_async_remote_copy(
            proj.at[which, rows], proj.at[which, rows], q_send.at[which, p], q_recv.at[which, p],
            device_id=other_side, device_id_type=MESH)

    far = jnp.maximum(pair, PAIRS - 1 - pair)

    def chain(which, t):
        @pl.when((t >= 0) & (t < PIECES))
        def _():
            rows = pl.ds(pl.multiple_of(t * PIECE, PIECE), PIECE)
            theirs = pl.ds(pl.multiple_of((1 - side) * SHARE + t * PIECE, PIECE), PIECE)
            out_p[which, rows] = own[which, theirs].astype(BF16)
            give(which, t).start()

        m = t - MERGED

        @pl.when((m >= 0) & (m < PIECES))
        def _():
            give(which, m).wait_recv()
            rows = pl.ds(pl.multiple_of(m * PIECE, PIECE), PIECE)
            own[which, mine_at(m)] += pair_in[which, rows].astype(F32)

        p = m - pair * SKEW

        @pl.when((p >= 0) & (p < PIECES))
        def _():
            @pl.when(pair > 0)
            def _():
                right(which, p).wait_recv()

            @pl.when(pair < PAIRS - 1)
            def _():
                rows = pl.ds(pl.multiple_of(p * PIECE, PIECE), PIECE)
                out_r[which, rows] = (own[which, mine_at(p)] + pre[which, rows].astype(F32)).astype(BF16)
                right(which, p).start()

        q = m - (PAIRS - 1 - pair) * SKEW

        @pl.when((q >= 0) & (q < PIECES))
        def _():
            @pl.when(pair < PAIRS - 1)
            def _():
                left(which, q).wait_recv()

            @pl.when(pair > 0)
            def _():
                rows = pl.ds(pl.multiple_of(q * PIECE, PIECE), PIECE)
                out_l[which, rows] = (own[which, mine_at(q)] + suf[which, rows].astype(F32)).astype(BF16)
                left(which, q).start()

        e = m - far * SKEW

        @pl.when((e >= 0) & (e < PIECES))
        def _():
            rows = pl.ds(pl.multiple_of(e * PIECE, PIECE), PIECE)
            proj[which, mine_at(e)] = (
                own[which, mine_at(e)] + (pre[which, rows].astype(F32) + suf[which, rows].astype(F32))).astype(BF16)
            share(which, e).start()

    btf[224:, :] = jnp.zeros((8, 128), F32)

    def swap_terms(which, z, x):
        rows = pl.ds(x * 4, 4)
        return pltpu.make_async_remote_copy(
            btb.at[which, 1 - core, z, rows], cbuf.at[which, z, rows], t_send.at[which, z, x], t_recv.at[which, z, x],
            device_id=other_core, device_id_type=MESH)

    def turn_of(i):
        return (lax.rem(1 - zh + i // 4, 2), lax.rem(xx + 1 + i, 4))

    def all_shared(which):
        def arrived(p, _):
            shared(which, p).wait_recv()
            return 0

        lax.fori_loop(0, PIECES, arrived, 0)

    mine_half = pl.ds(pl.multiple_of(side * SHARE, 128), SHARE)
    their_half = pl.ds(pl.multiple_of((1 - side) * SHARE, 128), SHARE)

    def early_terms(which):
        def body(i, _):
            rows = pl.ds(pl.multiple_of(i * 448, 32), 448)
            early[rows, :] = jnp.dot(got[rows, mine_half], proj[which, mine_half], preferred_element_type=F32)
            return 0

        lax.fori_loop(0, 4, body, 0)

    def terms_of(which):
        def terms(i, _):
            z, x = turn_of(i)
            first = pl.multiple_of(x * 448 + z * 224, 32)
            rows = pl.ds(first, 224)
            btf[0:224, :] = early[rows, :] + jnp.dot(got[rows, their_half], proj[which, their_half], preferred_element_type=F32)
            for k in range(4):
                two = btf[56 * k : 56 * k + 64, :]
                btb[which, 0, z, x * 4 + k] = two[:PAD].astype(BF16)
                btb[which, 1, z, x * 4 + k] = pltpu.roll(two, 64 - OWNED, 0)[:PAD].astype(BF16)
            swap_terms(which, z, x).start()
            return 0

        return terms

    def make_terms(which):
        early_terms(which)
        all_shared(which)
        lax.fori_loop(0, 8, terms_of(which), 0)

    def send_terms(which, z, q):
        return pltpu.make_async_remote_copy(
            s1.at[which, z, q], rb.at[which, z, pos], b_send.at[which, z, q], b_recv.at[which, z, pos],
            device_id=at_pos(q), device_id_type=MESH)

    def send_both(which, q):
        return pltpu.make_async_remote_copy(
            s1.at[which, pl.ds(0, 2), q], rb.at[which, pl.ds(0, 2), pos], b_send.at[which, 0, q], b_recv.at[which, 0, pos],
            device_id=at_pos(q), device_id_type=MESH)

    def add_cores_first(which):
        def body(i, _):
            x = lax.rem(xx + 1 + i, 4)
            for z in range(2):
                swap_terms(which, z, x).wait()
            for k in range(4):
                q = x * 4 + lax.rem(y + 1 + k, 4)
                for z in range(2):
                    s1[which, z, q] = (btb[which, core, z, q].astype(F32) + cbuf[which, z, q].astype(F32)).astype(BF16)

                @pl.when(q != pos)
                def _():
                    send_both(which, q).start()

            return 0

        lax.fori_loop(0, 4, body, 0)

    def make_and_add(which):
        terms = terms_of(which)

        def body(step, _):
            @pl.when(step < 8)
            def _():
                terms(step, 0)

            @pl.when(step >= BEHIND)
            def _():
                add(step - BEHIND)

            return 0

        def add(i):
            z, x = turn_of(i)
            swap_terms(which, z, x).wait()
            for k in range(4):
                q = x * 4 + lax.rem(y + 1 + k, 4)
                s1[which, z, q] = (btb[which, core, z, q].astype(F32) + cbuf[which, z, q].astype(F32)).astype(BF16)

                @pl.when(q != pos)
                def _():
                    send_terms(which, z, q).start()

        early_terms(which)
        all_shared(which)
        lax.fori_loop(0, 8 + BEHIND, body, 0)

    first_done = MERGED + far * SKEW + PIECES + (far - 2) * MERGED + (3 - far) * (LATER + 1)

    def step(t, _):
        chain(zh, t)
        chain(1 - zh, t - LATER)

        @pl.when(t == GATHERED)
        def _():
            each_peer(lambda i: wait_block(1 - zh, i))
            swap_core(1 - zh).start()

        @pl.when(t == PROJECTED)
        def _():
            swap_core(1 - zh).wait()
            unfold(1 - zh)
            project(1 - zh)

        @pl.when(t == first_done)
        def _():
            make_terms(zh)

        @pl.when(t == first_done + ADDED)
        def _():
            add_cores_first(zh)

        return 0

    lax.fori_loop(0, LATER + MERGED + (PAIRS - 1) * SKEW + PIECES + ADDED, step, 0)
    make_and_add(1 - zh)

    def swap_sum(which):
        return pltpu.make_async_remote_copy(
            zsend.at[which], zrecv.at[which], z_send.at[1 + which], z_recv.at[1 + which],
            device_id=other_zh, device_id_type=MESH)

    def add_chips(which, z):
        def body(i, acc):
            q = lax.rem(pos + 16 - i, 16)
            pltpu.make_async_remote_copy(
                s1.at[which, z, q], rb.at[which, z, q], b_send.at[which, z, q], b_recv.at[which, z, q],
                device_id=at_pos(q), device_id_type=MESH).wait_recv()
            return acc + rb[which, z, q].astype(F32)

        return lax.fori_loop(1, 16, body, s1[which, z, pos].astype(F32))

    def add_chips_first(which):
        def body(i, acc):
            q = lax.rem(pos + 16 - i, 16)
            pltpu.make_async_remote_copy(
                s1.at[which, pl.ds(0, 2), q], rb.at[which, pl.ds(0, 2), q], b_send.at[which, 0, q], b_recv.at[which, 0, q],
                device_id=at_pos(q), device_id_type=MESH).wait_recv()
            return (acc[0] + rb[which, zh, q].astype(F32), acc[1] + rb[which, 1 - zh, q].astype(F32))

        return lax.fori_loop(1, 16, body, (s1[which, zh, pos].astype(F32), s1[which, 1 - zh, pos].astype(F32)))

    mine, theirs = add_chips_first(zh)
    total[zh] = mine
    zsend[zh] = theirs.astype(BF16)
    swap_sum(zh).start()
    zsend[1 - zh] = add_chips(1 - zh, 1 - zh).astype(BF16)
    swap_sum(1 - zh).start()
    total[1 - zh] = add_chips(1 - zh, zh)
    swap_sum(zh).wait()
    swap_sum(1 - zh).wait()
    grad_sub = to_natural(jnp.concatenate([total[h] + zrecv[h].astype(F32) for h in range(2)], axis=1))[:OWNED]

    _, _, direction = adam_direction(grad_sub, mom[...], sec[...])
    grad[...] = grad_sub
    direct[OWNED - 4 :, :] = jnp.zeros((PAD - OWNED + 4, RANK), F32)
    direct[:OWNED, :] = to_halves(direction)
    dirs[f] = direct[...].astype(BF16)

    def send_dir(i):
        return pltpu.make_async_remote_copy(
            dirs.at[f], dirs.at[f], d_send.at[i], d_recv.at[f],
            device_id=(d, lax.rem(f + i, LINE)), device_id_type=MESH)

    def each_line(action):
        def body(i, _):
            action(i)
            return 0
        lax.fori_loop(1, LINE, body, 0)

    down = (LINE - 1 - f) // (LINE // 2)

    def start_dir(j, _):
        q = j + down * (LINE - 1 - 2 * j)

        @pl.when(q != f)
        def _():
            send_dir(lax.rem(q - f + LINE, LINE)).start()

        return 0

    lax.fori_loop(0, LINE, start_dir, 0)

    def wait_dir(i):
        q = lax.rem(f + LINE - i, LINE)
        pltpu.make_async_remote_copy(
            dirs.at[q], dirs.at[q], d_send.at[i], d_recv.at[q], device_id=(d, q), device_id_type=MESH).wait_recv()

    each_line(wait_dir)
    both = basis[...].reshape(RANK, FEATURES)
    row = lax.broadcasted_iota(jnp.int32, (OWNED * LINE, LINE * PAD), 0)
    col = lax.broadcasted_iota(jnp.int32, (OWNED * LINE, LINE * PAD), 1)
    order = jnp.where(col == (row % LINE) * PAD + row // LINE, 1.0, 0.0).astype(BF16)
    ordered = jnp.dot(order, dirs[...].reshape(LINE * PAD, RANK), preferred_element_type=F32).astype(BF16)
    upd[...] = jnp.dot(ordered, both, preferred_element_type=F32).astype(BF16)

    swap_zh.wait_send()
    each_line(lambda i: send_dir(i).wait_send())
    each_peer(lambda i: send_both(zh, lax.rem(pos + i, 16)).wait_send())
    for z in range(2):
        each_peer(lambda i: send_terms(1 - zh, z, lax.rem(pos + i, 16)).wait_send())
    for which in range(2):
        each_peer(lambda i: send_block(which, i).wait_send())

        def sent(p, _):
            give(which, p).wait_send()
            share(which, p).wait_send()

            @pl.when(pair < PAIRS - 1)
            def _():
                right(which, p).wait_send()

            @pl.when(pair > 0)
            def _():
                left(which, p).wait_send()

            return 0

        lax.fori_loop(0, PIECES, sent, 0)


def local(inputs, grad_out, projector, moment, second):
    blk = projector.T.reshape(4, 8, 128).transpose(1, 0, 2).reshape(32, 128)
    vmem = pl.BlockSpec(memory_space=pltpu.VMEM)
    anywhere = pl.BlockSpec(memory_space=pl.ANY)
    dma = pltpu.SemaphoreType.DMA
    update, grad_sub = pl.pallas_call(
        kernel,
        out_shape=(
            jax.ShapeDtypeStruct((OWNED * LINE, FEATURES), BF16),
            jax.ShapeDtypeStruct((OWNED, RANK), F32),
        ),
        in_specs=[anywhere, anywhere, anywhere, anywhere, anywhere],
        out_specs=(vmem, vmem),
        scratch_shapes=[
            pltpu.VMEM((TOKENS, FEATURES), BF16),
            pltpu.VMEM((TOKENS, UNITS), BF16),
            pltpu.VMEM((OWNED, RANK), F32),
            pltpu.VMEM((OWNED, RANK), F32),
            pltpu.VMEM((UNITS, TOKENS), BF16),
            pltpu.VMEM((2, 2, 16, 32, 128), BF16),
            pltpu.VMEM((2, 128, FEATURES), BF16),
            pltpu.VMEM((2, TOKENS, 128), F32),
            pltpu.VMEM((2, SHARE, 128), BF16),
            pltpu.VMEM((2, SHARE, 128), BF16),
            pltpu.VMEM((2, SHARE, 128), BF16),
            pltpu.VMEM((2, SHARE, 128), BF16),
            pltpu.VMEM((2, SHARE, 128), BF16),
            pltpu.VMEM((2, SHARE, 128), BF16),
            pltpu.VMEM((2, TOKENS, 128), BF16),
            pltpu.VMEM((UNITS, 128), F32),
            pltpu.VMEM((232, 128), F32),
            pltpu.VMEM((2, 2, 2, 16, PAD, 128), BF16),
            pltpu.VMEM((2, 2, 16, PAD, 128), BF16),
            pltpu.VMEM((2, 2, 16, PAD, 128), BF16),
            pltpu.VMEM((2, 2, 16, PAD, 128), BF16),
            pltpu.VMEM((2, PAD, 128), BF16),
            pltpu.VMEM((2, PAD, 128), BF16),
            pltpu.VMEM((2, PAD, 128), F32),
            pltpu.VMEM((PAD, RANK), F32),
            pltpu.VMEM((LINE, PAD, RANK), BF16),
            dma((5,)),
            dma((3,)), dma((3,)),
            dma((2, 16)), dma((2, 16)),
            dma((2,)), dma((2,)),
            dma((2, PIECES)), dma((2, PIECES)), dma((2, PIECES)), dma((2, PIECES)),
            dma((2, 2, 16)), dma((2, 2, 16)),
            dma((LINE,)), dma((LINE,)),
            dma((2, 2, 4)), dma((2, 2, 4)),
            dma((2, PIECES)), dma((2, PIECES)), dma((2, PIECES)), dma((2, PIECES)),
        ],
        compiler_params=pltpu.CompilerParams(
            collective_id=0, has_side_effects=True, vmem_limit_bytes=48 * 1024 * 1024),
    )(*[pltpu.with_memory_space_constraint(v, pltpu.HBM) for v in (blk, inputs, grad_out, moment, second)])
    moment_new, second_new, _ = adam_direction(grad_sub, moment, second)
    return (update.reshape(OWNED, LINE, FEATURES).transpose(1, 0, 2), moment_new, second_new)


def solution(mesh):
    return jax.shard_map(
        local,
        mesh=mesh,
        in_specs=(
            P("dp", "fsdp"),
            P("dp", "fsdp"),
            P("fsdp", "dp"),
            P(("fsdp", "dp"), None),
            P(("fsdp", "dp"), None),
        ),
        out_specs=(P(None, "dp", "fsdp"), P(("fsdp", "dp"), None), P(("fsdp", "dp"), None)),
        check_vma=False,
    )
```
